256 devices in a mesh: section: 8 (over z), dp: 32 (over x, y, core).
Axes of the slice: x: 4, y: 4, z: 8, core: 2. Of those that a mesh axis runs over, the one named last changes fastest.
Arguments:
- out_grad: bfloat16 [2, 2048, 6144], P(None, 'dp'), may hold values from -6 to 6
- x_rows: bfloat16 [8, 2, 64, 6144], P('section'), may hold values from -6 to 6
- saved_u: bfloat16 [8, 2, 64, 5376], P('section', None, None, 'dp'), may hold values from -6 to 6
- w_up_t: bfloat16 [8, 5376, 6144], P('section', 'dp'), may hold values from -0.078125 to 0.078125
- w_down: bfloat16 [8, 5376, 6144], P('section', 'dp'), may hold values from -0.078125 to 0.078125
- gate: float32 [8, 2, 64], P('section', None, 'dp'), may hold values from 0.2 to 1
- route_tokens: int32 [8, 2, 64], P('section', None, 'dp'), may hold values from 0 to 63
- route_count: int32 [8, 2, 32], P('section', None, 'dp'), may hold values from 1 to 2, as said below
Outputs:
- in_grad: bfloat16 [8, 2, 2048, 6144], P('section', None, 'dp')
- grad_up_t: bfloat16 [8, 5376, 6144], P('section', 'dp')
- grad_down: bfloat16 [8, 5376, 6144], P('section', 'dp')
The draws below stay inside these ranges and needn't reach their ends.
Inputs may be any that keep to these rules, and one draw needn't show every extreme that they name: `route_tokens`: a token index within the micro-batch rows of the slot's dp index. `route_count`: in every layer and micro-batch some dp index has all 2 slots live.
All inputs are finite; a program needn't handle non-finite values.
Results may differ from the reference program's by a relative error of at most 0.0059.
Values may be sent and summed in bfloat16 or wider, within the bound.
No kernel may reach another device: no remote copies, remote signals or barrier semaphores. Data moves between devices by JAX's collectives and lax.ppermute only.
A program may use at most 64 MiB of HBM per device.

```python
import math
import jax
import jax.numpy as jnp

D = 6144
HID = 5376
TOK_MB = 64
MICRO = 2
CAP = 2
LAYERS = 8
TOKENS = 2048
ROWS = 64
N_SECTION = 8
N_DP = 32


def draw_route_count(key, part):
    key = jax.random.fold_in(key, 5)
    first_key, second_key = jax.random.split(key)
    counts = jax.random.randint(first_key, (N_SECTION, MICRO, N_DP), 1, CAP + 1)
    filled = jax.random.randint(second_key, (N_SECTION, MICRO, 1), 0, N_DP)
    positions = jnp.arange(N_DP)[None, None, :]
    return jnp.where(positions == filled, CAP, counts).astype(jnp.int32)


def place_ends(drawn, own_key, low, largest):
    place = [jax.random.randint(jax.random.fold_in(own_key, axis), (), 0, length) for axis, length in enumerate(drawn.shape)]
    main_axis = drawn.shape.index(max(drawn.shape))
    neighbour = place[:main_axis] + [(place[main_axis] + 1) % drawn.shape[main_axis]] + place[main_axis + 1:]
    return drawn.at[tuple(place)].set(low).at[tuple(neighbour)].set(largest)


def steps_of(own_key, shape, pieces, least, largest):
    gain = 1.0
    for position, blocks in pieces:
        heights = jax.random.uniform(jax.random.fold_in(jax.random.fold_in(own_key, 6), position), (blocks,), jnp.float32, least / len(pieces), largest / len(pieces))
        gain = gain * jnp.repeat(jnp.exp(heights), shape[position] // blocks).reshape((-1,) + (1,) * (len(shape) - 1 - position))
    return gain


def scatter_about(stream_key, shape, deviation, most, shards=(), held_as=jnp.bfloat16):
    values = jax.random.normal(stream_key, shape, jnp.float32) * deviation
    if len(shards) > 0:
        values = steps_of(stream_key, shape, shards, -0.22, 0.18) * values
    return jnp.clip(values, min=-most, max=most).astype(held_as)


def setup_inputs(seed: int = 0) -> dict:
    keys = jax.random.split(jax.random.key(seed), 9)
    return {
        "out_grad": scatter_about(keys[0], (MICRO, TOKENS, D), 1.0, 6.0, ((1, 32),)),
        "x_rows": scatter_about(keys[1], (LAYERS, MICRO, ROWS, D), 1.0, 6.0, ((0, 8),)),
        "saved_u": scatter_about(keys[2], (LAYERS, MICRO, ROWS, HID), 1.5, 6.0, ((0, 8), (3, 32))),
        "w_up_t": scatter_about(keys[3], (LAYERS, HID, D), D ** -0.5, 0.078125, ((0, 8), (1, 32))),
        "w_down": scatter_about(keys[4], (LAYERS, HID, D), HID ** -0.5, 0.078125, ((0, 8), (1, 32))),
        "gate": jnp.clip(jnp.exp(math.log(1.0) - 1.609438 * jax.random.uniform(keys[5], (LAYERS, MICRO, ROWS), jnp.float32) ** steps_of(keys[5], (LAYERS, MICRO, ROWS), ((0, 8), (2, 32)), -0.2, 0.2)), 0.2, 1.0),
        "route_tokens": place_ends(jax.random.randint(keys[6], (LAYERS, MICRO, ROWS), 0, TOK_MB), jax.random.fold_in(keys[6], 1), 0, TOK_MB - 1).astype(jnp.int32),
        "route_count": draw_route_count(jax.random.fold_in(keys[8], 71), 0),
    }


def silu_pair(pre_activation):
    sigmoid_v = jax.nn.sigmoid(pre_activation)
    return pre_activation * sigmoid_v, sigmoid_v * (1.0 + pre_activation * (1.0 - sigmoid_v))


def reference(out_grad, x_rows, saved_u, w_up_t, w_down, gate, route_tokens, route_count):
    slot_index = jnp.arange(ROWS, dtype=jnp.int32)
    owner_index = slot_index // CAP
    slabs = [out_grad[micro_index] for micro_index in range(MICRO)]
    in_grads = []
    ups = []
    downs = []
    for layer_index in range(LAYERS - 1, -1, -1):
        grad_down = jnp.zeros((HID, D), jnp.float32)
        grad_up = jnp.zeros((HID, D), jnp.float32)
        layer_grads = []
        for micro_index in range(MICRO):
            grad_slab = slabs[micro_index]
            token_ids = (owner_index * TOK_MB + route_tokens[layer_index, micro_index]).astype(jnp.int32)
            live_slots = (slot_index % CAP) < route_count[layer_index, micro_index][owner_index]
            weights = jnp.where(live_slots, gate[layer_index, micro_index], jnp.float32(0.0))
            scaled = (weights[:, None] * grad_slab[token_ids].astype(jnp.float32)).astype(jnp.bfloat16)
            activation_f, slope_factor = silu_pair(saved_u[layer_index, micro_index].astype(jnp.float32))
            activation = activation_f.astype(jnp.bfloat16)
            hidden_back = jnp.dot(scaled, w_down[layer_index].T, preferred_element_type=jnp.float32)
            hidden_grad = (hidden_back * slope_factor).astype(jnp.bfloat16)
            grad_down = grad_down + jnp.dot(activation.T, scaled, preferred_element_type=jnp.float32)
            grad_up = grad_up + jnp.dot(hidden_grad.T, x_rows[layer_index, micro_index], preferred_element_type=jnp.float32)
            row_grad = jnp.dot(hidden_grad, w_up_t[layer_index], preferred_element_type=jnp.float32)
            updated = grad_slab.astype(jnp.float32).at[token_ids].add(row_grad)
            slabs[micro_index] = updated.astype(jnp.bfloat16)
            layer_grads.append(slabs[micro_index])
        in_grads.append(jnp.stack(layer_grads))
        ups.append(grad_up.astype(jnp.bfloat16))
        downs.append(grad_down.astype(jnp.bfloat16))
    in_grads = in_grads[::-1]
    ups = ups[::-1]
    downs = downs[::-1]
    return jnp.stack(in_grads), jnp.stack(ups), jnp.stack(downs)
```

```python
import jax
import jax.numpy as jnp
from jax import lax
from jax.sharding import PartitionSpec as P

BF = jnp.bfloat16
F32 = jnp.float32
LANES = 128


def per_device(out_grad, x_rows, saved_u, w_up_t, w_down, gate, route_tokens, route_count):
    section_count = lax.axis_size("section")
    dp_count = lax.axis_size("dp")
    section_index = lax.axis_index("section")
    core = lax.axis_index("dp") % 2
    micro_count, tok_rows, width = out_grad.shape
    cap = gate.shape[2]
    hid = w_down.shape[1]
    chips = dp_count // 2
    slots = micro_count * cap
    same_core = [[2 * chip + c for chip in range(chips)] for c in range(2)]
    sibling = [(i, i ^ 1) for i in range(dp_count)]
    down = w_down[0]
    up = w_up_t[0]

    def spread(block, axis, count, groups=None):
        sent = jnp.broadcast_to(block[None], (count,) + block.shape)
        return lax.all_to_all(sent, axis, 0, 0, tiled=True, axis_index_groups=groups)

    tokens = route_tokens[0]
    live = jnp.arange(cap)[None, :] < route_count[0]
    weights = jnp.where(live, gate[0], jnp.float32(0.0)).reshape(slots)
    slot_micro = jnp.arange(slots) // cap
    token_flat = tokens.reshape(slots)
    live_flat = live.reshape(slots)
    pick = (slot_micro * tok_rows + token_flat)[:, None] == jnp.arange(micro_count * tok_rows)[None, :]
    first_rows = jnp.dot(
        pick.astype(BF), out_grad.reshape(micro_count * tok_rows, width), preferred_element_type=F32
    )
    twin = (
        (slot_micro[:, None] == slot_micro[None, :])
        & (token_flat[:, None] == token_flat[None, :])
        & live_flat[None, :]
    ).astype(F32)

    view = saved_u[0].reshape(micro_count, chips, 2, cap, hid).transpose(2, 1, 0, 3, 4)
    view = jnp.where(core == 0, view, view[::-1]).reshape(dp_count * slots, hid).astype(F32)
    sigmoid_v = jax.nn.sigmoid(view)
    activation = (view * sigmoid_v).astype(BF)
    slope = sigmoid_v * (1.0 + view * (1.0 - sigmoid_v))

    lanes = jnp.arange(LANES)

    def one_round(row_in, dp_note, section_note):
        scaled = (weights[:, None] * row_in).astype(BF)
        sent = jnp.concatenate([scaled, dp_note], axis=1)
        own = spread(sent, "dp", chips, same_core)
        other = lax.ppermute(own, "dp", sibling)
        gathered = jnp.stack([own, other])
        rows = gathered[..., :width].reshape(dp_count * slots, width)
        back = jnp.einsum("rd,hd->rh", rows, down, preferred_element_type=F32)
        hidden_grad = (back * slope).astype(BF)
        partial = jnp.dot(hidden_grad, up, preferred_element_type=F32)
        partial = partial.reshape(2, chips, slots, width)
        arrived = lax.ppermute(partial[1].astype(BF), "dp", sibling)
        pair_sum = (partial[0] + arrived.astype(F32)).astype(BF)
        swapped = lax.all_to_all(pair_sum, "dp", 0, 0, tiled=True, axis_index_groups=same_core)
        row_grad = jnp.sum(swapped.astype(F32), axis=0)
        total = jnp.dot(twin, row_grad, precision=lax.Precision.HIGHEST)
        new_rows = (row_in + total).astype(BF)
        news = spread(jnp.concatenate([new_rows, section_note], axis=1), "section", section_count)
        return rows, hidden_grad, news, gathered[..., width:]

    blank = jnp.zeros((slots, LANES), BF)
    note = jnp.where(lanes[None, :] == 0, token_flat[:, None], jnp.where(lanes[None, :] == 1, live_flat[:, None], 0)).astype(BF)
    rows, hidden_grad, news, _ = one_round(first_rows, blank, note)

    all_tokens = news[:, :, width].astype(jnp.int32).reshape(section_count, micro_count, cap)
    all_live = news[:, :, width + 1].astype(jnp.int32).reshape(section_count, micro_count, cap) > 0
    layer = jnp.arange(section_count)

    token_ids = jnp.arange(tok_rows)
    touched = jnp.any(
        (all_tokens[..., None] == token_ids) & all_live[..., None], axis=2
    )
    depth = jnp.max(jnp.sum(touched.astype(jnp.int32), axis=0))

    def last_touch(allowed):
        ids = jnp.where(touched & allowed[:, None, None], layer[:, None, None], section_count)
        return jnp.min(ids, axis=0)

    above = last_touch(layer > section_index)
    upto = last_touch(layer >= section_index)

    def source(last):
        match = (
            (last[:, :, None, None] == layer[None, None, :, None])
            & (all_tokens.transpose(1, 0, 2)[:, None] == token_ids[None, :, None, None])
            & all_live.transpose(1, 0, 2)[:, None]
        )
        first = match & (jnp.cumsum(match.astype(jnp.int32), axis=3) == 1)
        return first.astype(BF)

    eye = jnp.eye(micro_count, dtype=BF)
    above_source = source(above)
    own_pick = pick.reshape(slots, micro_count, tok_rows).astype(BF)
    slot_source = jnp.einsum("rmt,mtls->rlms", own_pick, above_source).reshape(slots, section_count * slots)
    has_source = jnp.sum(slot_source.astype(F32), axis=1, keepdims=True) > 0

    def next_rows(news):
        table = news[..., :width].reshape(section_count * slots, width)
        return jnp.where(has_source, jnp.dot(slot_source, table, preferred_element_type=F32), first_rows)

    depth_note = jnp.broadcast_to(depth.astype(BF), (slots, LANES))
    rows, hidden_grad, news, notes = one_round(next_rows(news), depth_note, blank)
    rounds = jnp.max(notes.astype(F32)).astype(jnp.int32)

    def more(state):
        return state[0] < rounds

    def again(state):
        rows, hidden_grad, news, _ = one_round(next_rows(state[3]), blank, blank)
        return (state[0] + 1, rows, hidden_grad, news)

    _, rows, hidden_grad, news = lax.while_loop(more, again, (jnp.int32(2), rows, hidden_grad, news))

    upto_source = jnp.einsum("mtls,mn->mtlns", source(upto), eye).reshape(
        micro_count, tok_rows, section_count * slots
    )
    touched_here = upto < section_count
    table = news[..., :width].reshape(section_count * slots, width)
    moved = jnp.einsum("mtk,kd->mtd", upto_source, table, preferred_element_type=F32)
    in_grad = jnp.where(touched_here[:, :, None], moved.astype(BF), out_grad)

    grad_down = jnp.einsum("rh,rd->hd", activation, rows, preferred_element_type=F32).astype(BF)
    ordered = hidden_grad.reshape(2, chips, micro_count, cap, hid)
    ordered = jnp.where(core == 0, ordered, ordered[::-1]).transpose(2, 1, 0, 3, 4)
    grad_up = jnp.einsum(
        "rh,rd->hd",
        ordered.reshape(micro_count * dp_count * cap, hid),
        x_rows[0].reshape(micro_count * dp_count * cap, width),
        preferred_element_type=F32,
    ).astype(BF)
    return (in_grad[None], grad_up[None], grad_down[None])


def solution(mesh):
    return jax.shard_map(
        per_device,
        mesh=mesh,
        in_specs=(
            P(None, "dp", None),
            P("section", None, None, None),
            P("section", None, None, "dp"),
            P("section", "dp", None),
            P("section", "dp", None),
            P("section", None, "dp"),
            P("section", None, "dp"),
            P("section", None, "dp"),
        ),
        out_specs=(
            P("section", None, "dp", None),
            P("section", "dp", None),
            P("section", "dp", None),
        ),
        check_vma=False,
    )
```

```python
import jax
import jax.numpy as jnp
from jax import lax
from jax.experimental import pallas as pl
from jax.experimental.pallas import tpu as pltpu
from jax.sharding import PartitionSpec as P

BF = jnp.bfloat16
F32 = jnp.float32
I32 = jnp.int32
LANES = 128
LATE = 2


def plan_kernel(sections, cap, tok_rows, info_ref, place_ref, round_ref, own_ref, source_ref, ready_ref, last_ref):
    slots = 2 * cap
    place = place_ref[0]
    rows = 2 * tok_rows

    def clear(t, carry):
        ready_ref[t] = 1
        last_ref[t] = -1
        return carry

    lax.fori_loop(0, rows, clear, 0)
    row_ids = lax.broadcasted_iota(I32, source_ref.shape, 0)
    source_ref[...] = jnp.full(source_ref.shape, -1, I32)

    def layer_step(step, most):
        layer = sections - 1 - step
        at = (layer ^ place) * (2 * slots)
        token = [info_ref[at + i] + (i // cap) * tok_rows for i in range(slots)]
        live = [info_ref[at + slots + i] for i in range(slots)]
        own = layer == place
        for i in range(slots):
            prior = last_ref[token[i]]
            own_ref[i] = jnp.where(own, prior, own_ref[i])
        given = []
        for i in range(slots):
            twin_before = jnp.int32(0)
            twin_after = jnp.int32(0)
            for k in range((i // cap) * cap, (i // cap) * cap + cap):
                same = jnp.where((token[k] == token[i]) & (live[k] > 0), 1, 0)
                if k < i:
                    twin_before = jnp.maximum(twin_before, same * given[k])
                elif k > i:
                    twin_after = twin_after + same
            when = ready_ref[token[i]]
            size = 1 + twin_after
            for _ in range(slots - 1):
                taken = jnp.int32(0)
                for k in range(i):
                    taken = taken + jnp.where(given[k] == when, 1, 0)
                when = jnp.where((when >= 2) & (taken + size > LATE), when + 1, when)
            when = jnp.where(twin_before > 0, twin_before, when)
            when = jnp.where(live[i] > 0, when, 0)
            given.append(when)
        for i in range(slots):
            round_ref[layer * slots + i] = given[i]
            most = jnp.maximum(most, given[i])
            ready_ref[token[i]] = jnp.where(live[i] > 0, given[i] + 1, ready_ref[token[i]])
            last_ref[token[i]] = jnp.where(live[i] > 0, layer * slots + i, last_ref[token[i]])
            hit = (row_ids == token[i]) & ((live[i] > 0) & (layer >= place))
            source_ref[...] = jnp.where(hit, layer * slots + i, source_ref[...])
        return most

    for i in range(slots):
        own_ref[i] = -1
    own_ref[slots] = lax.fori_loop(0, sections, layer_step, jnp.int32(1))


def plan(info, place, sections, cap, tok_rows):
    slots = 2 * cap
    smem = pl.BlockSpec(memory_space=pltpu.SMEM)
    return pl.pallas_call(
        lambda *refs: plan_kernel(sections, cap, tok_rows, *refs),
        in_specs=[smem, smem],
        out_specs=[smem, smem, pl.BlockSpec(memory_space=pltpu.VMEM)],
        out_shape=[
            jax.ShapeDtypeStruct((sections * slots,), I32),
            jax.ShapeDtypeStruct((slots + 1,), I32),
            jax.ShapeDtypeStruct((2 * tok_rows, LANES), I32),
        ],
        scratch_shapes=[pltpu.SMEM((2 * tok_rows,), I32), pltpu.SMEM((2 * tok_rows,), I32)],
        cost_estimate=pl.CostEstimate(flops=100000, bytes_accessed=70000, transcendentals=0),
    )(info, place)


def per_device(out_grad, x_rows, saved_u, w_up_t, w_down, gate, route_tokens, route_count):
    section_count = lax.axis_size("section")
    dp_count = lax.axis_size("dp")
    section_index = lax.axis_index("section")
    core = lax.axis_index("dp") % 2
    micro_count, tok_rows, width = out_grad.shape
    cap = gate.shape[2]
    hid = w_down.shape[1]
    chips = dp_count // 2
    slots = micro_count * cap
    same_core = [[2 * chip + c for chip in range(chips)] for c in range(2)]
    sibling = [(i, i ^ 1) for i in range(dp_count)]
    down = w_down[0]
    up = w_up_t[0]
    flat_out = out_grad.reshape(micro_count * tok_rows, width)

    def spread(block, axis, count, groups=None):
        sent = jnp.broadcast_to(block[None], (count,) + block.shape)
        return lax.all_to_all(sent, axis, 0, 0, tiled=True, axis_index_groups=groups)

    token_flat = route_tokens[0].reshape(slots)
    live = (jnp.arange(cap)[None, :] < route_count[0]).reshape(slots)
    weights = jnp.where(live, gate[0].reshape(slots), jnp.float32(0.0))
    slot_micro = jnp.arange(slots) // cap

    info = jnp.concatenate([token_flat, live.astype(I32)])[None]
    hop = 1
    while hop < section_count:
        arrived = lax.ppermute(info, "section", [(i, i ^ hop) for i in range(section_count)])
        info = jnp.concatenate([info, arrived])
        hop *= 2
    rounds_of, own_plan, source = plan(info.reshape(-1), section_index.reshape(1), section_count, cap, tok_rows)
    own_round = lax.dynamic_slice(rounds_of, (section_index * slots,), (slots,))
    own_source = own_plan[:slots]

    pick = (slot_micro * tok_rows + token_flat)[:, None] == jnp.arange(micro_count * tok_rows)[None, :]
    first_rows = jnp.dot(pick.astype(BF), flat_out, preferred_element_type=F32)
    twin = (
        (slot_micro[:, None] == slot_micro[None, :]) & (token_flat[:, None] == token_flat[None, :]) & live[None, :]
    ).astype(F32)

    view = saved_u[0].reshape(micro_count, chips, 2, cap, hid).transpose(2, 1, 0, 3, 4)
    view = jnp.where(core == 0, view, view[::-1]).reshape(dp_count, slots, hid).astype(F32)
    sigmoid_v = jax.nn.sigmoid(view)
    activation = (view * sigmoid_v).astype(BF)
    slope = sigmoid_v * (1.0 + view * (1.0 - sigmoid_v))

    def gather(sent):
        own = spread(sent, "dp", chips, same_core)
        other = lax.ppermute(own, "dp", sibling)
        return jnp.concatenate([own, other])

    def layer_pass(rows, slopes):
        count = rows.shape[1]
        back = jnp.einsum("rd,hd->rh", rows.reshape(dp_count * count, width), down, preferred_element_type=F32)
        hidden_grad = (back.reshape(dp_count, count, hid) * slopes).astype(BF)
        partial = jnp.dot(hidden_grad.reshape(dp_count * count, hid), up, preferred_element_type=F32)
        partial = partial.reshape(2, chips, count, width)
        arrived = lax.ppermute(partial[1].astype(BF), "dp", sibling)
        pair_sum = (partial[0] + arrived.astype(F32)).astype(BF)
        swapped = lax.all_to_all(pair_sum, "dp", 0, 0, tiled=True, axis_index_groups=same_core)
        return hidden_grad, jnp.sum(swapped.astype(F32), axis=0)

    rows = gather((weights[:, None] * first_rows).astype(BF))
    hidden_grad, row_grad = layer_pass(rows, slope)
    total = jnp.sum(twin[:, :, None] * row_grad[None], axis=1)
    new_rows = (first_rows + total).astype(BF)
    table = spread(new_rows, "section", section_count).reshape(section_count * slots, width)
    first_bf = first_rows.astype(BF)

    lanes = jnp.arange(LANES)
    late = jnp.arange(LATE)
    table_ids = jnp.arange(section_count * slots)

    def chosen(rounds, now):
        mine = rounds == now
        rank = jnp.cumsum(mine.astype(I32), axis=-1) - 1
        return mine[..., None, :] & (rank[..., None, :] == late[:, None])

    def send_rows(now, table):
        which = chosen(own_round, now)
        weight = jnp.sum(jnp.where(which, weights, 0.0), axis=1)
        from_table = jnp.any(which[:, :, None] & (own_source[:, None] == table_ids)[None], axis=1)
        from_first = which & (own_source < 0)[None, :]
        row_in = jnp.dot(from_table.astype(BF), table, preferred_element_type=F32) + jnp.dot(
            from_first.astype(BF), first_bf, preferred_element_type=F32
        )
        return which, row_in, (weight[:, None] * row_in).astype(BF)

    def finish(now, which, row_in, late_rows, all_rounds, rows, hidden_grad):
        taken = chosen(all_rounds, now)
        late_slope = jnp.sum(jnp.where(taken[..., None], slope[:, None], 0.0), axis=2)
        late_hidden, row_grad = layer_pass(late_rows, late_slope)
        for c in range(LATE):
            rows = jnp.where(taken[:, c, :, None], late_rows[:, c : c + 1], rows)
            hidden_grad = jnp.where(taken[:, c, :, None], late_hidden[:, c : c + 1], hidden_grad)
        paired = jnp.any(which[:, None, :, None] & which[None, :, None, :] & (twin > 0)[None, None], axis=(2, 3))
        new_rows = row_in
        for c in range(LATE):
            new_rows = new_rows + jnp.where(paired[:, c : c + 1], row_grad[c : c + 1], 0.0)
        return new_rows.astype(BF), rows, hidden_grad

    def take_in(now, new_rows, table):
        news = spread(new_rows, "section", section_count)
        sent = chosen(rounds_of.reshape(section_count, slots), now)
        table = table.reshape(section_count, slots, width)
        for c in range(LATE):
            table = jnp.where(sent[:, c, :, None], news[:, c : c + 1], table)
        return table.reshape(section_count * slots, width)

    which, row_in, scaled = send_rows(2, table)
    word = jnp.sum(jnp.where(lanes[None, :] == jnp.arange(slots + 1)[:, None], jnp.concatenate([own_round, own_plan[slots:]])[:, None], 0), axis=0)
    word = jnp.broadcast_to(word.astype(BF), (LATE, LANES))
    got = gather(jnp.concatenate([scaled, word], axis=1))
    words = got[:, 0, width:].astype(F32).astype(I32)
    all_rounds = words[:, :slots]
    rounds = jnp.max(words[:, slots])
    new_rows, rows, hidden_grad = finish(2, which, row_in, got[..., :width], all_rounds, rows, hidden_grad)

    def more(state):
        return state[0] < rounds

    def again(state):
        done, new_rows, table, rows, hidden_grad = state
        table = take_in(done, new_rows, table)
        now = done + 1
        which, row_in, scaled = send_rows(now, table)
        late_rows = gather(scaled)
        new_rows, rows, hidden_grad = finish(now, which, row_in, late_rows, all_rounds, rows, hidden_grad)
        return now, new_rows, table, rows, hidden_grad

    done, new_rows, table, rows, hidden_grad = lax.while_loop(
        more, again, (jnp.int32(2), new_rows, table, rows, hidden_grad)
    )
    table = take_in(done, new_rows, table)

    grad_down = jnp.einsum(
        "rh,rd->hd",
        activation.reshape(dp_count * slots, hid),
        rows.reshape(dp_count * slots, width),
        preferred_element_type=F32,
    ).astype(BF)
    ordered = hidden_grad.reshape(2, chips, micro_count, cap, hid)
    ordered = jnp.where(core == 0, ordered, ordered[::-1]).transpose(2, 1, 0, 3, 4)
    grad_up = jnp.einsum(
        "rh,rd->hd",
        ordered.reshape(micro_count * dp_count * cap, hid),
        x_rows[0].reshape(micro_count * dp_count * cap, width),
        preferred_element_type=F32,
    ).astype(BF)
    moved = jnp.dot(
        (source[:, : section_count * slots] == table_ids[None, :]).astype(BF), table, preferred_element_type=F32
    )
    in_grad = jnp.where(source[:, :1] >= 0, moved.astype(BF), flat_out).reshape(out_grad.shape)
    return (in_grad[None], grad_up[None], grad_down[None])


def solution(mesh):
    return jax.shard_map(
        per_device,
        mesh=mesh,
        in_specs=(
            P(None, "dp", None),
            P("section", None, None, None),
            P("section", None, None, "dp"),
            P("section", "dp", None),
            P("section", "dp", None),
            P("section", None, "dp"),
            P("section", None, "dp"),
            P("section", None, "dp"),
        ),
        out_specs=(
            P("section", None, "dp", None),
            P("section", "dp", None),
            P("section", "dp", None),
        ),
        check_vma=False,
    )
```

```python
import functools

import jax
import jax.numpy as jnp
from jax import lax
from jax.experimental import pallas as pl
from jax.experimental.pallas import tpu as pltpu
from jax.sharding import PartitionSpec as P

BF = jnp.bfloat16
F32 = jnp.float32
I32 = jnp.int32
LANES = 128
LATE = 2
NT = (((1,), (1,)), ((), ()))
TN = (((0,), (0,)), ((), ()))
SMEM = pl.BlockSpec(memory_space=pltpu.SMEM)
VMEM = pl.BlockSpec(memory_space=pltpu.VMEM)


def call(kernel, ins, outs, out_specs, scratch=(), flops=1000000, size=1000000):
    return pl.pallas_call(
        kernel,
        in_specs=ins,
        out_specs=out_specs,
        out_shape=outs,
        scratch_shapes=list(scratch),
        compiler_params=pltpu.CompilerParams(vmem_limit_bytes=40 * 1024 * 1024),
        cost_estimate=pl.CostEstimate(flops=flops, bytes_accessed=size, transcendentals=0),
    )


def chunks(width):
    step = next(s for s in (1024, 768, 512, 384, 256, 128) if width % s == 0)
    return [pl.ds(at, step) for at in range(0, width, step)]


def dot(a, b, dims=None):
    if dims is None:
        return jnp.dot(a, b, preferred_element_type=F32)
    return lax.dot_general(a, b, dims, preferred_element_type=F32)


def iota(shape, axis):
    return lax.broadcasted_iota(I32, shape, axis)


def one_hot(flag):
    return jnp.where(flag, 1.0, 0.0).astype(BF)


def column(values, shape):
    rows = iota(shape, 0)
    out = jnp.full(shape, values[0])
    for i in range(1, len(values)):
        out = jnp.where(rows == i, values[i], out)
    return out


def first_kernel(token_ref, count_ref, gate_ref, grad_ref, sent_ref, first_ref, info_ref):
    micros, tok_rows, width = grad_ref.shape
    cap = token_ref.shape[2]
    slots = micros * cap
    tokens = [token_ref[0, i // cap, i % cap] for i in range(slots)]
    live = [jnp.where(i % cap < count_ref[0, i // cap, 0], 1, 0) for i in range(slots)]
    weights = [jnp.where(live[i] > 0, gate_ref[0, i // cap, i % cap], 0.0) for i in range(slots)]
    lane = iota((1, LANES), 1)
    info = jnp.zeros((1, LANES), I32)
    for i in range(slots):
        info = jnp.where(lane == i, tokens[i], info)
        info = jnp.where(lane == slots + i, live[i], info)
    info_ref[...] = info
    wanted = column([tokens[i] + (i // cap) * tok_rows for i in range(slots)], (8, micros * tok_rows))
    pick = one_hot(wanted == iota(wanted.shape, 1))
    weight = column(weights, (8, LANES))[:, :1]
    for part in chunks(width):
        rows = dot(pick, grad_ref[:, :, part].reshape(micros * tok_rows, part.size))
        first_ref[:, part] = rows[:slots].astype(BF)
        scaled = (weight * rows)[:slots].astype(BF)
        for chip in range(sent_ref.shape[0]):
            sent_ref[chip, :, part] = scaled


def plan_kernel(sections, cap, tok_rows, info_ref, place_ref, round_ref, own_ref, source_ref, ready_ref, last_ref):
    slots = 2 * cap
    place = place_ref[0]
    rows = 2 * tok_rows

    def clear(t, carry):
        ready_ref[t] = 1
        last_ref[t] = -1
        return carry

    lax.fori_loop(0, rows, clear, 0)
    row_ids = iota(source_ref.shape, 0)
    source_ref[...] = jnp.full(source_ref.shape, -1, I32)

    def layer_step(step, most):
        layer = sections - 1 - step
        at = layer ^ place
        token = [info_ref[at, i] + (i // cap) * tok_rows for i in range(slots)]
        live = [info_ref[at, slots + i] for i in range(slots)]
        own = layer == place
        for i in range(slots):
            prior = last_ref[token[i]]
            own_ref[i] = jnp.where(own, prior, own_ref[i])
        given = []
        for i in range(slots):
            twin_before = jnp.int32(0)
            twin_after = jnp.int32(0)
            for k in range((i // cap) * cap, (i // cap) * cap + cap):
                same = jnp.where((token[k] == token[i]) & (live[k] > 0), 1, 0)
                if k < i:
                    twin_before = jnp.maximum(twin_before, same * given[k])
                elif k > i:
                    twin_after = twin_after + same
            when = ready_ref[token[i]]
            size = 1 + twin_after
            for _ in range(slots - 1):
                taken = jnp.int32(0)
                for k in range(i):
                    taken = taken + jnp.where(given[k] == when, 1, 0)
                when = jnp.where((when >= 2) & (taken + size > LATE), when + 1, when)
            when = jnp.where(twin_before > 0, twin_before, when)
            when = jnp.where(live[i] > 0, when, 0)
            given.append(when)
        for i in range(slots):
            round_ref[layer * slots + i] = given[i]
            most = jnp.maximum(most, given[i])
            ready_ref[token[i]] = jnp.where(live[i] > 0, given[i] + 1, ready_ref[token[i]])
            last_ref[token[i]] = jnp.where(live[i] > 0, layer * slots + i, last_ref[token[i]])
            hit = (row_ids == token[i]) & ((live[i] > 0) & (layer >= place))
            source_ref[...] = jnp.where(hit, layer * slots + i, source_ref[...])
        return most

    for i in range(slots):
        own_ref[i] = -1
    own_ref[slots] = lax.fori_loop(0, sections, layer_step, jnp.int32(1))


def row_map(round_ref, sections, slots, now):
    found = []
    for layer in range(sections):
        rank = jnp.int32(0)
        for i in range(slots):
            hit = round_ref[layer * slots + i] == now
            found.append(jnp.where(hit, sections * slots + layer * LATE + rank, layer * slots + i))
            rank = rank + jnp.where(hit, 1, 0)
    return found


def own_picks(round_ref, place, slots, now):
    picks = [jnp.int32(-1)] * LATE
    rank = jnp.int32(0)
    for i in range(slots):
        hit = round_ref[place * slots + i] == now
        for c in range(LATE):
            picks[c] = jnp.where(hit & (rank == c), i, picks[c])
        rank = rank + jnp.where(hit, 1, 0)
    return picks


def send_kernel(fresh, note, cap, now_ref, place_ref, round_ref, own_ref, gate_ref, first_ref, table_ref, *refs):
    refs = list(refs)
    news_ref = refs.pop(0) if fresh else None
    sent_ref, row_in_ref = refs.pop(0), refs.pop(0)
    merged_ref = refs.pop(0) if fresh else None
    map_ref = refs.pop(0)
    sections, slots, width = table_ref.shape
    known = sections * slots
    now, place = now_ref[0], place_ref[0]
    if fresh:
        where_is = row_map(round_ref, sections, slots, now - 1)
    else:
        where_is = [jnp.int32(k) for k in range(known)]
    for k in range(known):
        map_ref[k] = where_is[k]
    wanted, from_first, weights = [], [], []
    for slot in own_picks(round_ref, place, slots, now):
        at = jnp.maximum(slot, 0)
        source = own_ref[at]
        wanted.append(jnp.where((slot >= 0) & (source >= 0), map_ref[jnp.maximum(source, 0)], -1))
        from_first.append(jnp.where((slot >= 0) & (source < 0), slot, -1))
        weights.append(jnp.where(slot >= 0, gate_ref[0, at // cap, at % cap], 0.0))
    weight = column(weights, (8, LANES))[:, :1]
    first_id = column(from_first + [jnp.int32(-1)], (8, LANES))
    in_first = [jnp.where(first_id == i, 1.0, 0.0)[:, :1] for i in range(slots)]
    old_ids = column(wanted + [jnp.int32(-1)], (8, known))
    pick_old = one_hot(old_ids == iota(old_ids.shape, 1))
    if fresh:
        extra = sections * LATE
        new_ids = column(wanted + [jnp.int32(-1)], (8, extra))
        pick_new = one_hot(new_ids == iota(new_ids.shape, 1) + known)
        keep_old = one_hot(column(where_is, (known, known)) == iota((known, known), 1))
        take_new = one_hot(column(where_is, (known, extra)) == iota((known, extra), 1) + known)
    for part in chunks(width):
        old = table_ref[:, :, part].reshape(known, part.size)
        rows = dot(pick_old, old)
        if fresh:
            new = news_ref[:, :, part].reshape(extra, part.size)
            rows = rows + dot(pick_new, new)
            merged = dot(keep_old, old) + dot(take_new, new)
            merged_ref[:, :, part] = merged.astype(BF).reshape(sections, slots, part.size)
        first = first_ref[:, part].astype(F32)
        for i in range(slots):
            rows = rows + in_first[i] * first[i : i + 1]
        row_in_ref[:, part] = rows[:LATE]
        scaled = (weight * rows)[:LATE].astype(BF)
        for chip in range(sent_ref.shape[0]):
            sent_ref[chip, :, part] = scaled
    if note:
        lane = iota((LATE, LANES), 1)
        word = jnp.zeros((LATE, LANES), I32)
        for i in range(slots):
            word = jnp.where(lane == i, round_ref[place * slots + i], word)
        word = jnp.where(lane == slots, own_ref[slots], word).astype(F32).astype(BF)
        for chip in range(sent_ref.shape[0]):
            sent_ref[chip, :, pl.ds(width, LANES)] = word


def places(count, chips, cap, tok_group, core, taken=None):
    total = 2 * chips * count
    row = iota((total, LANES), 0)
    half = row // (chips * count)
    chip = (row // count) % chips
    index = chip * 2 + (core ^ half)
    if taken is None:
        slot = row % count
        return (slot // cap) * tok_group + index * cap + slot % cap
    place = jnp.full((total, LANES), -1, I32)
    for i, flag in enumerate(taken):
        place = jnp.where(flag, (i // cap) * tok_group + index * cap + i % cap, place)
    return place


def pass_kernel(count, late, cap, core_ref, now_ref, saved_ref, down_ref, up_ref, own_ref, other_ref, *refs):
    refs = list(refs)
    note_in = refs.pop(0) if late == 2 else None
    mine_ref, theirs_ref, hidden_ref = refs[:3]
    chips = own_ref.shape[0]
    micros, group, hid = saved_ref.shape[1:]
    width = mine_ref.shape[2]
    half = chips * count
    core = core_ref[0]
    taken = None
    if late:
        if late == 1:
            perm_ref, note_ref, most_ref = refs[3:]
            word = jnp.concatenate(
                [own_ref[:, :, pl.ds(width, LANES)].reshape(half, LANES), other_ref[:, :, pl.ds(width, LANES)].reshape(half, LANES)]
            ).astype(F32)
            note_ref[...] = word
            most_ref[0] = jnp.max(word).astype(I32)
        else:
            (perm_ref,) = refs[3:]
            word = note_in[...]
        now = now_ref[0].astype(F32)
        position = (iota((2 * half, 1), 0) % count).astype(F32)
        rank = jnp.zeros((2 * half, 1), F32)
        taken = []
        for i in range(micros * cap):
            hit = jnp.where(word[:, i : i + 1] == now, 1.0, 0.0)
            flag = jnp.where(rank == position, hit, 0.0)
            taken.append(jnp.broadcast_to(flag, (2 * half, LANES)) > 0.5)
            rank = rank + hit
    place = places(count, chips, cap, group, core, taken)
    perm = one_hot(place == iota(place.shape, 1))
    if late:
        perm_ref[...] = perm
    v = dot(perm, saved_ref[0].reshape(micros * group, hid))
    s = 1.0 / (1.0 + jnp.exp(-v))
    slope = s * (1.0 + v * (1.0 - s))
    back = jnp.zeros((2 * half, hid), F32)
    for part in chunks(width):
        rows = jnp.concatenate(
            [own_ref[:, :, part].reshape(half, part.size), other_ref[:, :, part].reshape(half, part.size)]
        )
        back = back + dot(rows, down_ref[0, :, part], NT)
    hidden = (back * slope).astype(BF)
    hidden_ref[...] = hidden
    for part in chunks(width):
        partial = dot(hidden, up_ref[0, :, part])
        mine_ref[:, :, part] = partial[:half].reshape(chips, count, part.size)
        theirs_ref[:, :, part] = partial[half:].astype(BF).reshape(chips, count, part.size)


def news_kernel(late, cap, now_ref, place_ref, round_ref, token_ref, row_in_ref, swapped_ref, news_ref):
    chips, count, width = swapped_ref.shape
    slots = token_ref.shape[1] * cap
    ids = own_picks(round_ref, place_ref[0], slots, now_ref[0]) if late else list(range(count))
    micro, token = [], []
    for c, slot in enumerate(ids):
        at = jnp.maximum(slot, 0)
        micro.append(jnp.where(slot >= 0, at // cap, -1 - c))
        token.append(token_ref[0, at // cap, at % cap])
    twins = []
    for b in range(count):
        same = [
            jnp.where((micro[a] == micro[b]) & (token[a] == token[b]), 1.0, 0.0) if a != b else jnp.float32(0.0)
            for a in range(count)
        ]
        twins.append(column(same, (count, LANES))[:, :1])
    for part in chunks(width):
        own = swapped_ref[0, :, part].astype(F32)
        for chip in range(1, chips):
            own = own + swapped_ref[chip, :, part].astype(F32)
        total = own
        for b in range(count):
            total = total + twins[b] * own[b : b + 1]
        rows = (row_in_ref[:, part].astype(F32) + total).astype(BF)
        for section in range(news_ref.shape[0]):
            news_ref[section, :, part] = rows


def grads_kernel(cap, core_ref, saved_ref, saved_t_ref, x_ref, hid1, hid2, hid3, perm2, perm3, own1, other1, own2, other2, own3, other3, up_ref, down_ref):
    micros, group, hid = saved_ref.shape[1:]
    natural = micros * group
    chips, slots, width = own1.shape
    place = places(slots, chips, cap, group, core_ref[0])
    perm1 = one_hot(place == iota(place.shape, 1))
    late = jnp.concatenate([perm2[...], perm3[...]])
    later = dot(one_hot(iota((8, late.shape[0]), 0) >= 0), late)[:1]
    masked1 = jnp.where(later > 0.5, 0.0, perm1.astype(F32)).astype(BF)
    perms = jnp.concatenate([masked1, late])
    v = saved_t_ref[...].astype(F32)
    act = (v * (1.0 / (1.0 + jnp.exp(-v)))).astype(BF)
    act_rows = dot(act, perms, NT).astype(BF)
    hidden = jnp.concatenate([hid1[...], hid2[...], hid3[...]])
    hidden_t = dot(hidden, perms, TN).astype(BF)
    for part in chunks(width):
        rows = jnp.concatenate(
            [r[:, :, part].reshape(chips * r.shape[1], part.size) for r in (own1, other1, own2, other2, own3, other3)]
        )
        down_ref[0, :, part] = dot(act_rows, rows).astype(BF)
        up_ref[0, :, part] = dot(hidden_t, x_ref[0, :, :, part].reshape(natural, part.size)).astype(BF)


def output_kernel(last_ref, round_ref, source_ref, grad_ref, table_ref, news_ref, out_ref):
    sections, slots, width = table_ref.shape
    known, extra = sections * slots, sections * LATE
    micros, tok_rows, _ = grad_ref.shape
    where_is = row_map(round_ref, sections, slots, last_ref[0])
    keep_old = one_hot(column(where_is, (known, known)) == iota((known, known), 1))
    take_new = one_hot(column(where_is, (known, extra)) == iota((known, extra), 1) + known)
    source = source_ref[...]
    chosen = one_hot(source[:, :known] == iota((micros * tok_rows, known), 1))
    from_old = dot(chosen, keep_old).astype(BF)
    from_new = dot(chosen, take_new).astype(BF)
    still = jnp.where(source < 0, 1.0, 0.0)[:, :1]
    for part in chunks(width):
        moved = dot(from_old, table_ref[:, :, part].reshape(known, part.size))
        moved = moved + dot(from_new, news_ref[:, :, part].reshape(extra, part.size))
        kept = grad_ref[:, :, part].reshape(micros * tok_rows, part.size).astype(F32)
        rows = (moved + still * kept).astype(BF)
        out_ref[0, :, :, part] = rows.reshape(micros, tok_rows, part.size)


def per_device(out_grad, x_rows, saved_u, w_up_t, w_down, gate, route_tokens, route_count):
    sections = lax.axis_size("section")
    dp_count = lax.axis_size("dp")
    section_index = lax.axis_index("section")
    core = lax.axis_index("dp") % 2
    micros, tok_rows, width = out_grad.shape
    cap = gate.shape[2]
    hid = w_down.shape[1]
    chips = dp_count // 2
    slots = micros * cap
    same_core = [[2 * chip + c for chip in range(chips)] for c in range(2)]
    sibling = [(i, i ^ 1) for i in range(dp_count)]
    place = section_index.reshape(1).astype(I32)
    core_id = core.reshape(1).astype(I32)

    def shape(dims, dtype):
        return jax.ShapeDtypeStruct(dims, dtype)

    def swap(block, axis, groups=None):
        return lax.all_to_all(block, axis, 0, 0, tiled=True, axis_index_groups=groups)

    def hop_along(info, distance):
        arrived = lax.ppermute(info, "section", [(i, i ^ distance) for i in range(sections)])
        return jnp.concatenate([info, arrived])

    def send(now, fresh, note, table, news=None):
        wide = width + (LANES if note else 0)
        outs = [shape((chips, LATE, wide), BF), shape((LATE, width), F32)]
        outs += [shape(table.shape, BF)] if fresh else []
        return call(
            functools.partial(send_kernel, fresh, note, cap),
            [SMEM] * 5 + [VMEM] * (3 if fresh else 2),
            outs,
            [VMEM] * len(outs),
            [pltpu.SMEM((sections * slots,), I32)],
        )(now, place, rounds_of, own_plan, gate, first, table, *([news] if fresh else []))

    def one_pass(now, late, own, note=None, tie=None):
        other = lax.ppermute(own, "dp", sibling)
        count = own.shape[1]
        total = 2 * chips * count
        outs = [shape((chips, count, width), F32), shape((chips, count, width), BF), shape((total, hid), BF)]
        specs = [VMEM] * 3
        if late:
            outs.append(shape((total, LANES), BF))
            specs.append(VMEM)
        if late == 1:
            outs += [shape((total, LANES), F32), shape((1,), I32)]
            specs += [VMEM, SMEM]
        mine, theirs, *rest = call(
            functools.partial(pass_kernel, count, late, cap),
            [SMEM, SMEM] + [VMEM] * (5 + (late == 2)),
            outs,
            specs,
            flops=4 * total * hid * width,
            size=4 * hid * width + 8 * total * width,
        )(core_id, now, saved_u, w_down, w_up_t, own, other, *([note] if late == 2 else []))
        if tie is not None:
            theirs, tied = lax.optimization_barrier((theirs, tie))
            rest.append(tied)
        arrived = lax.ppermute(theirs, "dp", sibling)
        pair_sum = (mine + arrived.astype(F32)).astype(BF)
        return other, swap(pair_sum, "dp", same_core), rest

    def make_news(now, late, row_in, swapped):
        return call(
            functools.partial(news_kernel, late, cap),
            [SMEM] * 4 + [VMEM] * 2,
            shape((sections,) + swapped.shape[1:], BF),
            VMEM,
        )(now, place, rounds_of if late else place, route_tokens, row_in, swapped)

    def number(n):
        return jnp.full((1,), n, I32)

    sent, first, info = call(
        first_kernel,
        [SMEM] * 3 + [VMEM],
        [shape((chips, slots, width), BF), shape((slots, width), BF), shape((1, LANES), I32)],
        [VMEM] * 3,
    )(route_tokens, route_count, gate, out_grad)
    hops = [1 << k for k in range(sections.bit_length() - 1)]
    info = hop_along(info, hops[0])
    own1 = swap(sent, "dp", same_core)
    info = hop_along(info, hops[1])
    own1, info = lax.optimization_barrier((own1, info))
    for distance in hops[2:]:
        info = hop_along(info, distance)
    other1, swapped, (hid1, info) = one_pass(number(1), 0, own1, tie=info)
    rounds_of, own_plan, source = call(
        functools.partial(plan_kernel, sections, cap, tok_rows),
        [SMEM, SMEM],
        [shape((sections * slots,), I32), shape((slots + 1,), I32), shape((micros * tok_rows, LANES), I32)],
        [SMEM, SMEM, VMEM],
        [pltpu.SMEM((micros * tok_rows,), I32)] * 2,
    )(info, place)
    table = swap(make_news(number(1), False, first, swapped), "section")

    sent, row_in = send(number(2), False, True, table)
    own2 = swap(sent, "dp", same_core)
    other2, swapped, (hid2, perm2, note, most) = one_pass(number(2), 1, own2)
    news = swap(make_news(number(2), True, row_in, swapped), "section")

    sent, row_in, table = send(number(3), True, False, table, news)
    own3 = swap(sent, "dp", same_core)
    other3, swapped, (hid3, perm3) = one_pass(number(3), 2, own3, note)
    news = make_news(number(3), True, row_in, swapped)

    def more(state):
        return state[0] < most[0]

    def again(state):
        done, news, table, own1, other1, hid1 = state
        now = (done + 1).reshape(1)
        sent, row_in, table = send(now, True, False, table, swap(news, "section"))
        own = swap(sent, "dp", same_core)
        other, swapped, (hidden, _) = one_pass(now, 2, own, note)
        news = make_news(now, True, row_in, swapped)
        hit = note[::LATE, :slots] == now[0].astype(F32)
        rank = jnp.cumsum(hit.astype(I32), axis=1) - 1
        hid1 = hid1.reshape(dp_count, slots, hid)
        hidden = hidden.reshape(dp_count, LATE, hid)
        for c in range(LATE):
            taken = (hit & (rank == c))[:, :, None]
            own1 = jnp.where(taken[:chips], own[:, c : c + 1], own1)
            other1 = jnp.where(taken[chips:], other[:, c : c + 1], other1)
            hid1 = jnp.where(taken, hidden[:, c : c + 1], hid1)
        return done + 1, news, table, own1, other1, hid1.reshape(dp_count * slots, hid)

    done, news, table, own1, other1, hid1 = lax.while_loop(
        more, again, (jnp.int32(3), news, table, own1, other1, hid1)
    )
    news = swap(news, "section")

    grad_up, grad_down = call(
        functools.partial(grads_kernel, cap),
        [SMEM] + [VMEM] * 14,
        [shape((1, hid, width), BF)] * 2,
        [VMEM] * 2,
        flops=8 * dp_count * slots * hid * width,
        size=8 * hid * width,
    )(
        core_id, saved_u, saved_u.reshape(micros * dp_count * cap, hid).T, x_rows,
        hid1, hid2, hid3, perm2, perm3, own1, other1, own2[..., :width], other2[..., :width], own3, other3,
    )
    in_grad = call(
        output_kernel,
        [SMEM, SMEM] + [VMEM] * 4,
        shape((1, micros, tok_rows, width), BF),
        VMEM,
    )(done.reshape(1), rounds_of, source, out_grad, table, news)
    return (in_grad, grad_up, grad_down)


def solution(mesh):
    return jax.shard_map(
        per_device,
        mesh=mesh,
        in_specs=(
            P(None, "dp", None),
            P("section", None, None, None),
            P("section", None, None, "dp"),
            P("section", "dp", None),
            P("section", "dp", None),
            P("section", None, "dp"),
            P("section", None, "dp"),
            P("section", None, "dp"),
        ),
        out_specs=(
            P("section", None, "dp", None),
            P("section", "dp", None),
            P("section", "dp", None),
        ),
        check_vma=False,
    )
```

```python
import functools

import jax
import jax.numpy as jnp
from jax import lax
from jax.experimental import pallas as pl
from jax.experimental.pallas import tpu as pltpu
from jax.sharding import PartitionSpec as P

BF = jnp.bfloat16
F32 = jnp.float32
I32 = jnp.int32
LANES = 128
LATE = 2
NT = (((1,), (1,)), ((), ()))
TN = (((0,), (0,)), ((), ()))
SMEM = pl.BlockSpec(memory_space=pltpu.SMEM)
VMEM = pl.BlockSpec(memory_space=pltpu.VMEM)


def call(kernel, ins, outs, out_specs, scratch=(), flops=1000000, size=1000000):
    return pl.pallas_call(
        kernel,
        in_specs=ins,
        out_specs=out_specs,
        out_shape=outs,
        scratch_shapes=list(scratch),
        compiler_params=pltpu.CompilerParams(vmem_limit_bytes=24 * 1024 * 1024),
        cost_estimate=pl.CostEstimate(flops=flops, bytes_accessed=size, transcendentals=0),
    )


def chunks(width):
    step = next(s for s in (1024, 768, 512, 384, 256, 128) if width % s == 0)
    return [pl.ds(at, step) for at in range(0, width, step)]


def dot(a, b, dims=None):
    if dims is None:
        return jnp.dot(a, b, preferred_element_type=F32)
    return lax.dot_general(a, b, dims, preferred_element_type=F32)


def iota(shape, axis):
    return lax.broadcasted_iota(I32, shape, axis)


def one_hot(flag):
    return jnp.where(flag, 1.0, 0.0).astype(BF)


def column(values, shape):
    rows = iota(shape, 0)
    out = jnp.full(shape, values[0])
    for i in range(1, len(values)):
        out = jnp.where(rows == i, values[i], out)
    return out


def first_kernel(token_ref, count_ref, gate_ref, grad_ref, sent_ref, first_ref, info_ref):
    micros, tok_rows, width = grad_ref.shape
    cap = token_ref.shape[2]
    slots = micros * cap
    tokens = [token_ref[0, i // cap, i % cap] for i in range(slots)]
    live = [jnp.where(i % cap < count_ref[0, i // cap, 0], 1, 0) for i in range(slots)]
    weights = [jnp.where(live[i] > 0, gate_ref[0, i // cap, i % cap], 0.0) for i in range(slots)]
    lane = iota((1, LANES), 1)
    info = jnp.zeros((1, LANES), I32)
    for i in range(slots):
        info = jnp.where(lane == i, tokens[i], info)
        info = jnp.where(lane == slots + i, live[i], info)
    info_ref[...] = info
    wanted = column([tokens[i] + (i // cap) * tok_rows for i in range(slots)], (8, micros * tok_rows))
    pick = one_hot(wanted == iota(wanted.shape, 1))
    weight = column(weights, (8, LANES))[:, :1]
    for part in chunks(width):
        rows = dot(pick, grad_ref[:, :, part].reshape(micros * tok_rows, part.size))
        first_ref[:, part] = rows[:slots].astype(BF)
        scaled = (weight * rows)[:slots].astype(BF)
        for chip in range(sent_ref.shape[0]):
            sent_ref[chip, :, part] = scaled


def plan_kernel(sections, cap, tok_rows, info_ref, place_ref, round_ref, own_ref, source_ref, ready_ref, last_ref):
    slots = 2 * cap
    place = place_ref[0]
    rows = 2 * tok_rows

    def clear(t, carry):
        ready_ref[t] = 1
        last_ref[t] = -1
        return carry

    lax.fori_loop(0, rows, clear, 0)
    row_ids = iota(source_ref.shape, 0)
    source_ref[...] = jnp.full(source_ref.shape, -1, I32)

    def layer_step(step, most):
        layer = sections - 1 - step
        at = layer ^ place
        token = [info_ref[at, i] + (i // cap) * tok_rows for i in range(slots)]
        live = [info_ref[at, slots + i] for i in range(slots)]
        own = layer == place
        for i in range(slots):
            prior = last_ref[token[i]]
            own_ref[i] = jnp.where(own, prior, own_ref[i])
        given = []
        for i in range(slots):
            twin_before = jnp.int32(0)
            twin_after = jnp.int32(0)
            for k in range((i // cap) * cap, (i // cap) * cap + cap):
                same = jnp.where((token[k] == token[i]) & (live[k] > 0), 1, 0)
                if k < i:
                    twin_before = jnp.maximum(twin_before, same * given[k])
                elif k > i:
                    twin_after = twin_after + same
            when = ready_ref[token[i]]
            size = 1 + twin_after
            for _ in range(slots - 1):
                taken = jnp.int32(0)
                for k in range(i):
                    taken = taken + jnp.where(given[k] == when, 1, 0)
                when = jnp.where((when >= 2) & (taken + size > LATE), when + 1, when)
            when = jnp.where(twin_before > 0, twin_before, when)
            when = jnp.where(live[i] > 0, when, 0)
            given.append(when)
        for i in range(slots):
            round_ref[layer * slots + i] = given[i]
            most = jnp.maximum(most, given[i])
            ready_ref[token[i]] = jnp.where(live[i] > 0, given[i] + 1, ready_ref[token[i]])
            last_ref[token[i]] = jnp.where(live[i] > 0, layer * slots + i, last_ref[token[i]])
            hit = (row_ids == token[i]) & ((live[i] > 0) & (layer >= place))
            source_ref[...] = jnp.where(hit, layer * slots + i, source_ref[...])
        return most

    for i in range(slots):
        own_ref[i] = -1
    own_ref[slots] = lax.fori_loop(0, sections, layer_step, jnp.int32(1))


def row_map(round_ref, sections, slots, now):
    found = []
    for layer in range(sections):
        rank = jnp.int32(0)
        for i in range(slots):
            hit = round_ref[layer * slots + i] == now
            found.append(jnp.where(hit, sections * slots + layer * LATE + rank, layer * slots + i))
            rank = rank + jnp.where(hit, 1, 0)
    return found


def own_picks(round_ref, place, slots, now):
    picks = [jnp.int32(-1)] * LATE
    rank = jnp.int32(0)
    for i in range(slots):
        hit = round_ref[place * slots + i] == now
        for c in range(LATE):
            picks[c] = jnp.where(hit & (rank == c), i, picks[c])
        rank = rank + jnp.where(hit, 1, 0)
    return picks


def send_kernel(fresh, note, cap, now_ref, place_ref, round_ref, own_ref, gate_ref, first_ref, table_ref, *refs):
    refs = list(refs)
    news_ref = refs.pop(0) if fresh else None
    sent_ref, row_in_ref = refs.pop(0), refs.pop(0)
    merged_ref = refs.pop(0) if fresh else None
    map_ref = refs.pop(0)
    sections, slots, width = table_ref.shape
    known = sections * slots
    now, place = now_ref[0], place_ref[0]
    if fresh:
        where_is = row_map(round_ref, sections, slots, now - 1)
    else:
        where_is = [jnp.int32(k) for k in range(known)]
    for k in range(known):
        map_ref[k] = where_is[k]
    wanted, from_first, weights = [], [], []
    for slot in own_picks(round_ref, place, slots, now):
        at = jnp.maximum(slot, 0)
        source = own_ref[at]
        wanted.append(jnp.where((slot >= 0) & (source >= 0), map_ref[jnp.maximum(source, 0)], -1))
        from_first.append(jnp.where((slot >= 0) & (source < 0), slot, -1))
        weights.append(jnp.where(slot >= 0, gate_ref[0, at // cap, at % cap], 0.0))
    weight = column(weights, (8, LANES))[:, :1]
    first_id = column(from_first + [jnp.int32(-1)], (8, LANES))
    in_first = [jnp.where(first_id == i, 1.0, 0.0)[:, :1] for i in range(slots)]
    old_ids = column(wanted + [jnp.int32(-1)], (8, known))
    pick_old = one_hot(old_ids == iota(old_ids.shape, 1))
    if fresh:
        extra = sections * LATE
        new_ids = column(wanted + [jnp.int32(-1)], (8, extra))
        pick_new = one_hot(new_ids == iota(new_ids.shape, 1) + known)
        keep_old = one_hot(column(where_is, (known, known)) == iota((known, known), 1))
        take_new = one_hot(column(where_is, (known, extra)) == iota((known, extra), 1) + known)
    for part in chunks(width):
        old = table_ref[:, :, part].reshape(known, part.size)
        rows = dot(pick_old, old)
        if fresh:
            new = news_ref[:, :, part].reshape(extra, part.size)
            rows = rows + dot(pick_new, new)
            merged = dot(keep_old, old) + dot(take_new, new)
            merged_ref[:, :, part] = merged.astype(BF).reshape(sections, slots, part.size)
        first = first_ref[:, part].astype(F32)
        for i in range(slots):
            rows = rows + in_first[i] * first[i : i + 1]
        row_in_ref[:, part] = rows[:LATE]
        scaled = (weight * rows)[:LATE].astype(BF)
        for chip in range(sent_ref.shape[0]):
            sent_ref[chip, :, part] = scaled
    if note:
        lane = iota((LATE, LANES), 1)
        word = jnp.zeros((LATE, LANES), I32)
        for i in range(slots):
            word = jnp.where(lane == i, round_ref[place * slots + i], word)
        word = jnp.where(lane == slots, own_ref[slots], word).astype(F32).astype(BF)
        for chip in range(sent_ref.shape[0]):
            sent_ref[chip, :, pl.ds(width, LANES)] = word


def places(count, chips, cap, tok_group, core, taken=None):
    total = 2 * chips * count
    row = iota((total, LANES), 0)
    half = row // (chips * count)
    chip = (row // count) % chips
    index = chip * 2 + (core ^ half)
    if taken is None:
        slot = row % count
        return (slot // cap) * tok_group + index * cap + slot % cap
    place = jnp.full((total, LANES), -1, I32)
    for i, flag in enumerate(taken):
        place = jnp.where(flag, (i // cap) * tok_group + index * cap + i % cap, place)
    return place


def pass_kernel(count, late, cap, core_ref, now_ref, saved_ref, down_ref, up_ref, own_ref, other_ref, *refs):
    refs = list(refs)
    note_in = refs.pop(0) if late == 2 else None
    mine_ref, theirs_ref, hidden_ref = refs[:3]
    chips = own_ref.shape[0]
    micros, group, hid = saved_ref.shape[1:]
    width = mine_ref.shape[2]
    half = chips * count
    core = core_ref[0]
    taken = None
    if late:
        if late == 1:
            perm_ref, note_ref, most_ref = refs[3:]
            word = jnp.concatenate(
                [own_ref[:, :, pl.ds(width, LANES)].reshape(half, LANES), other_ref[:, :, pl.ds(width, LANES)].reshape(half, LANES)]
            ).astype(F32)
            note_ref[...] = word
            most_ref[0] = jnp.max(word).astype(I32)
        else:
            (perm_ref,) = refs[3:]
            word = note_in[...]
        now = now_ref[0].astype(F32)
        position = (iota((2 * half, 1), 0) % count).astype(F32)
        rank = jnp.zeros((2 * half, 1), F32)
        taken = []
        for i in range(micros * cap):
            hit = jnp.where(word[:, i : i + 1] == now, 1.0, 0.0)
            flag = jnp.where(rank == position, hit, 0.0)
            taken.append(jnp.broadcast_to(flag, (2 * half, LANES)) > 0.5)
            rank = rank + hit
    place = places(count, chips, cap, group, core, taken)
    perm = one_hot(place == iota(place.shape, 1))
    if late:
        perm_ref[...] = perm
    v = dot(perm, saved_ref[0].reshape(micros * group, hid))
    s = 1.0 / (1.0 + jnp.exp(-v))
    slope = s * (1.0 + v * (1.0 - s))
    back = jnp.zeros((2 * half, hid), F32)
    for part in chunks(width):
        rows = jnp.concatenate(
            [own_ref[:, :, part].reshape(half, part.size), other_ref[:, :, part].reshape(half, part.size)]
        )
        back = back + dot(rows, down_ref[0, :, part], NT)
    hidden = (back * slope).astype(BF)
    hidden_ref[...] = hidden
    for part in chunks(width):
        partial = dot(hidden, up_ref[0, :, part])
        mine_ref[:, :, part] = partial[:half].reshape(chips, count, part.size)
        theirs_ref[:, :, part] = partial[half:].astype(BF).reshape(chips, count, part.size)


def news_kernel(late, cap, now_ref, place_ref, round_ref, token_ref, row_in_ref, swapped_ref, news_ref):
    chips, count, width = swapped_ref.shape
    slots = token_ref.shape[1] * cap
    ids = own_picks(round_ref, place_ref[0], slots, now_ref[0]) if late else list(range(count))
    micro, token = [], []
    for c, slot in enumerate(ids):
        at = jnp.maximum(slot, 0)
        micro.append(jnp.where(slot >= 0, at // cap, -1 - c))
        token.append(token_ref[0, at // cap, at % cap])
    twins = []
    for b in range(count):
        same = [
            jnp.where((micro[a] == micro[b]) & (token[a] == token[b]), 1.0, 0.0) if a != b else jnp.float32(0.0)
            for a in range(count)
        ]
        twins.append(column(same, (count, LANES))[:, :1])
    for part in chunks(width):
        own = swapped_ref[0, :, part].astype(F32)
        for chip in range(1, chips):
            own = own + swapped_ref[chip, :, part].astype(F32)
        total = own
        for b in range(count):
            total = total + twins[b] * own[b : b + 1]
        rows = (row_in_ref[:, part].astype(F32) + total).astype(BF)
        for section in range(news_ref.shape[0]):
            news_ref[section, :, part] = rows


def grads_kernel(cap, core_ref, saved_ref, saved_t_ref, x_ref, hid1, hid2, hid3, perm2, perm3, own1, other1, own2, other2, own3, other3, up_ref, down_ref):
    micros, group, hid = saved_ref.shape[1:]
    natural = micros * group
    chips, slots, width = own1.shape
    place = places(slots, chips, cap, group, core_ref[0])
    perm1 = one_hot(place == iota(place.shape, 1))
    late = jnp.concatenate([perm2[...], perm3[...]])
    later = dot(one_hot(iota((8, late.shape[0]), 0) >= 0), late)[:1]
    masked1 = jnp.where(later > 0.5, 0.0, perm1.astype(F32)).astype(BF)
    perms = jnp.concatenate([masked1, late])
    v = saved_t_ref[...].astype(F32)
    act = (v * (1.0 / (1.0 + jnp.exp(-v)))).astype(BF)
    act_rows = dot(act, perms, NT).astype(BF)
    hidden = jnp.concatenate([hid1[...], hid2[...], hid3[...]])
    hidden_t = dot(hidden, perms, TN).astype(BF)
    for part in chunks(width):
        rows = jnp.concatenate(
            [r[:, :, part].reshape(chips * r.shape[1], part.size) for r in (own1, other1, own2, other2, own3, other3)]
        )
        down_ref[0, :, part] = dot(act_rows, rows).astype(BF)
        up_ref[0, :, part] = dot(hidden_t, x_ref[0, :, :, part].reshape(natural, part.size)).astype(BF)


def output_kernel(last_ref, round_ref, source_ref, grad_ref, table_ref, news_ref, out_ref):
    sections, slots, width = table_ref.shape
    known, extra = sections * slots, sections * LATE
    micros, tok_rows, _ = grad_ref.shape
    where_is = row_map(round_ref, sections, slots, last_ref[0])
    keep_old = one_hot(column(where_is, (known, known)) == iota((known, known), 1))
    take_new = one_hot(column(where_is, (known, extra)) == iota((known, extra), 1) + known)
    source = source_ref[...]
    chosen = one_hot(source[:, :known] == iota((micros * tok_rows, known), 1))
    from_old = dot(chosen, keep_old).astype(BF)
    from_new = dot(chosen, take_new).astype(BF)
    still = jnp.where(source < 0, 1.0, 0.0)[:, :1]
    for part in chunks(width):
        moved = dot(from_old, table_ref[:, :, part].reshape(known, part.size))
        moved = moved + dot(from_new, news_ref[:, :, part].reshape(extra, part.size))
        kept = grad_ref[:, :, part].reshape(micros * tok_rows, part.size).astype(F32)
        rows = (moved + still * kept).astype(BF)
        out_ref[0, :, :, part] = rows.reshape(micros, tok_rows, part.size)


def per_device(out_grad, x_rows, saved_u, w_up_t, w_down, gate, route_tokens, route_count):
    sections = lax.axis_size("section")
    dp_count = lax.axis_size("dp")
    section_index = lax.axis_index("section")
    core = lax.axis_index("dp") % 2
    micros, tok_rows, width = out_grad.shape
    cap = gate.shape[2]
    hid = w_down.shape[1]
    chips = dp_count // 2
    slots = micros * cap
    same_core = [[2 * chip + c for chip in range(chips)] for c in range(2)]
    sibling = [(i, i ^ 1) for i in range(dp_count)]
    place = section_index.reshape(1).astype(I32)
    core_id = core.reshape(1).astype(I32)

    def shape(dims, dtype):
        return jax.ShapeDtypeStruct(dims, dtype)

    def swap(block, axis, groups=None):
        return lax.all_to_all(block, axis, 0, 0, tiled=True, axis_index_groups=groups)

    def hop_along(info, distance):
        arrived = lax.ppermute(info, "section", [(i, i ^ distance) for i in range(sections)])
        return jnp.concatenate([info, arrived])

    def send(now, fresh, note, table, news=None):
        wide = width + (LANES if note else 0)
        outs = [shape((chips, LATE, wide), BF), shape((LATE, width), F32)]
        outs += [shape(table.shape, BF)] if fresh else []
        return call(
            functools.partial(send_kernel, fresh, note, cap),
            [SMEM] * 5 + [VMEM] * (3 if fresh else 2),
            outs,
            [VMEM] * len(outs),
            [pltpu.SMEM((sections * slots,), I32)],
        )(now, place, rounds_of, own_plan, gate, first, table, *([news] if fresh else []))

    def one_pass(now, late, own, note=None, tie=None, beside=None):
        other = lax.ppermute(own, "dp", sibling)
        count = own.shape[1]
        total = 2 * chips * count
        outs = [shape((chips, count, width), F32), shape((chips, count, width), BF), shape((total, hid), BF)]
        specs = [VMEM] * 3
        if late:
            outs.append(shape((total, LANES), BF))
            specs.append(VMEM)
        if late == 1:
            outs += [shape((total, LANES), F32), shape((1,), I32)]
            specs += [VMEM, SMEM]
        mine, theirs, *rest = call(
            functools.partial(pass_kernel, count, late, cap),
            [SMEM, SMEM] + [VMEM] * (5 + (late == 2)),
            outs,
            specs,
            flops=4 * total * hid * width,
            size=4 * hid * width + 8 * total * width,
        )(core_id, now, saved_u, w_down, w_up_t, own, other, *([note] if late == 2 else []))
        arrived = lax.ppermute(theirs, "dp", sibling)
        pair_sum = (mine + arrived.astype(F32)).astype(BF)
        if beside is None:
            return other, swap(pair_sum, "dp", same_core), rest
        pair_sum, tie = lax.optimization_barrier((pair_sum, tie))
        swapped, *done = lax.optimization_barrier((swap(pair_sum, "dp", same_core), *beside(tie)))
        return other, swapped, rest, done

    def make_news(now, late, row_in, swapped):
        return call(
            functools.partial(news_kernel, late, cap),
            [SMEM] * 4 + [VMEM] * 2,
            shape((sections,) + swapped.shape[1:], BF),
            VMEM,
        )(now, place, rounds_of if late else place, route_tokens, row_in, swapped)

    def number(n):
        return jnp.full((1,), n, I32)

    sent, first, info = call(
        first_kernel,
        [SMEM] * 3 + [VMEM],
        [shape((chips, slots, width), BF), shape((slots, width), BF), shape((1, LANES), I32)],
        [VMEM] * 3,
    )(route_tokens, route_count, gate, out_grad)
    hops = [1 << k for k in range(sections.bit_length() - 1)]
    info = hop_along(info, hops[0])
    own1 = swap(sent, "dp", same_core)
    info = hop_along(info, hops[1])
    own1, info = lax.optimization_barrier((own1, info))

    def plan(info):
        for distance in hops[2:]:
            info = hop_along(info, distance)
        return call(
            functools.partial(plan_kernel, sections, cap, tok_rows),
            [SMEM, SMEM],
            [shape((sections * slots,), I32), shape((slots + 1,), I32), shape((micros * tok_rows, LANES), I32)],
            [SMEM, SMEM, VMEM],
            [pltpu.SMEM((micros * tok_rows,), I32)] * 2,
        )(info, place)

    other1, swapped, (hid1,), (rounds_of, own_plan, source) = one_pass(number(1), 0, own1, tie=info, beside=plan)
    table = swap(make_news(number(1), False, first, swapped), "section")

    sent, row_in = send(number(2), False, True, table)
    own2 = swap(sent, "dp", same_core)
    other2, swapped, (hid2, perm2, note, most) = one_pass(number(2), 1, own2)
    news = swap(make_news(number(2), True, row_in, swapped), "section")

    sent, row_in, table = send(number(3), True, False, table, news)
    own3 = swap(sent, "dp", same_core)
    other3, swapped, (hid3, perm3) = one_pass(number(3), 2, own3, note)
    news = make_news(number(3), True, row_in, swapped)

    def more(state):
        return state[0] < most[0]

    def again(state):
        done, news, table, own1, other1, hid1 = state
        now = (done + 1).reshape(1)
        sent, row_in, table = send(now, True, False, table, swap(news, "section"))
        own = swap(sent, "dp", same_core)
        other, swapped, (hidden, _) = one_pass(now, 2, own, note)
        news = make_news(now, True, row_in, swapped)
        hit = note[::LATE, :slots] == now[0].astype(F32)
        rank = jnp.cumsum(hit.astype(I32), axis=1) - 1
        hid1 = hid1.reshape(dp_count, slots, hid)
        hidden = hidden.reshape(dp_count, LATE, hid)
        for c in range(LATE):
            taken = (hit & (rank == c))[:, :, None]
            own1 = jnp.where(taken[:chips], own[:, c : c + 1], own1)
            other1 = jnp.where(taken[chips:], other[:, c : c + 1], other1)
            hid1 = jnp.where(taken, hidden[:, c : c + 1], hid1)
        return done + 1, news, table, own1, other1, hid1.reshape(dp_count * slots, hid)

    done, news, table, own1, other1, hid1 = lax.while_loop(
        more, again, (jnp.int32(3), news, table, own1, other1, hid1)
    )
    news = swap(news, "section")

    grad_up, grad_down = call(
        functools.partial(grads_kernel, cap),
        [SMEM] + [VMEM] * 14,
        [shape((1, hid, width), BF)] * 2,
        [VMEM] * 2,
        flops=8 * dp_count * slots * hid * width,
        size=8 * hid * width,
    )(
        core_id, saved_u, saved_u.reshape(micros * dp_count * cap, hid).T, x_rows,
        hid1, hid2, hid3, perm2, perm3, own1, other1, own2, other2, own3, other3,
    )
    in_grad = call(
        output_kernel,
        [SMEM, SMEM] + [VMEM] * 4,
        shape((1, micros, tok_rows, width), BF),
        VMEM,
    )(done.reshape(1), rounds_of, source, out_grad, table, news)
    return (in_grad, grad_up, grad_down)


def solution(mesh):
    return jax.shard_map(
        per_device,
        mesh=mesh,
        in_specs=(
            P(None, "dp", None),
            P("section", None, None, None),
            P("section", None, None, "dp"),
            P("section", "dp", None),
            P("section", "dp", None),
            P("section", None, "dp"),
            P("section", None, "dp"),
            P("section", None, "dp"),
        ),
        out_specs=(
            P("section", None, "dp", None),
            P("section", "dp", None),
            P("section", "dp", None),
        ),
        check_vma=False,
    )
```

```python
import functools

import jax
import jax.numpy as jnp
from jax import lax
from jax.experimental import pallas as pl
from jax.experimental.pallas import tpu as pltpu
from jax.sharding import PartitionSpec as P

BF = jnp.bfloat16
F32 = jnp.float32
I32 = jnp.int32
LANES = 128
ROOM = 2
UNROLLED = 3
NT = (((1,), (1,)), ((), ()))
TN = (((0,), (0,)), ((), ()))
SMEM = pl.BlockSpec(memory_space=pltpu.SMEM)
VMEM = pl.BlockSpec(memory_space=pltpu.VMEM)
ANY = pl.BlockSpec(memory_space=pl.ANY)


def call(kernel, ins, outs, out_specs, scratch=(), flops=1000000, size=1000000):
    return pl.pallas_call(
        kernel,
        in_specs=ins,
        out_specs=out_specs,
        out_shape=outs,
        scratch_shapes=list(scratch),
        compiler_params=pltpu.CompilerParams(vmem_limit_bytes=24 * 1024 * 1024),
        cost_estimate=pl.CostEstimate(flops=flops, bytes_accessed=size, transcendentals=0),
    )


def chunks(width):
    step = next(s for s in (1024, 768, 512, 384, 256, 128) if width % s == 0)
    return [pl.ds(at, step) for at in range(0, width, step)]


def dot(a, b, dims=None):
    if dims is None:
        return jnp.dot(a, b, preferred_element_type=F32)
    return lax.dot_general(a, b, dims, preferred_element_type=F32)


def iota(shape, axis):
    return lax.broadcasted_iota(I32, shape, axis)


def one_hot(flag):
    return jnp.where(flag, 1.0, 0.0).astype(BF)


def column(values, shape):
    rows = iota(shape, 0)
    out = jnp.full(shape, values[0])
    for i in range(1, len(values)):
        out = jnp.where(rows == i, values[i], out)
    return out


def info_kernel(token_ref, count_ref, info_ref):
    micros, cap = token_ref.shape[1:]
    slots = micros * cap
    lane = iota((1, LANES), 1)
    info = jnp.zeros((1, LANES), I32)
    for i in range(slots):
        live = jnp.where(i % cap < count_ref[0, 0, i // cap], 1, 0)
        info = jnp.where(lane == i, token_ref[0, i // cap, i % cap], info)
        info = jnp.where(lane == slots + i, live, info)
    for section in range(info_ref.shape[0]):
        info_ref[section] = info


def first_kernel(token_ref, grad_ref, first_ref):
    micros, tok_rows, width = grad_ref.shape
    cap = token_ref.shape[2]
    slots = micros * cap
    tokens = [token_ref[0, i // cap, i % cap] + (i // cap) * tok_rows for i in range(slots)]
    wanted = column(tokens, (8, micros * tok_rows))
    pick = one_hot(wanted == iota(wanted.shape, 1))
    for part in chunks(width):
        rows = dot(pick, grad_ref[:, :, part].reshape(micros * tok_rows, part.size))
        first_ref[:, part] = rows[:slots].astype(BF)


def plan_kernel(sections, cap, tok_rows, info_ref, place_ref, round_ref, own_ref, source_ref, round2_ref, own2_ref, ready_ref, last_ref, below_ref, height_ref):
    slots = 2 * cap
    place = place_ref[0]

    def routed(layer):
        token = [info_ref[layer, 0, i] + (i // cap) * tok_rows for i in range(slots)]
        live = [info_ref[layer, 0, slots + i] for i in range(slots)]
        return token, live

    def mates(i):
        return [k for k in range(i // cap * cap, i // cap * cap + cap) if k != i]

    def clear(layer, carry):
        for token in routed(layer)[0]:
            ready_ref[token] = 1
            last_ref[token] = -1
            below_ref[token] = 0
        return carry

    def climb(layer, carry):
        token, live = routed(layer)
        for i in range(slots):
            height_ref[layer * slots + i] = below_ref[token[i]]
        for i in range(slots):
            new = live[i]
            for k in mates(i):
                if k < i:
                    new = jnp.where((token[k] == token[i]) & (live[k] > 0), 0, new)
            below_ref[token[i]] = below_ref[token[i]] + new
        return carry

    def descend(step, most):
        layer = sections - 1 - step
        token, live = routed(layer)
        own = layer == place
        for i in range(slots):
            own_ref[i] = jnp.where(own, last_ref[token[i]], own_ref[i])
        height = [height_ref[layer * slots + i] for i in range(slots)]
        ready = [ready_ref[token[i]] for i in range(slots)]
        twin = [
            [(k, (token[k] == token[i]) & (live[k] > 0)) for k in mates(i)] for i in range(slots)
        ]
        given = [jnp.int32(0)] * slots
        for awaited in (True, False):
            for i in range(slots):
                wanted = (height[i] > 0) if awaited else (height[i] == 0)
                wanted = wanted & (live[i] > 0) & (given[i] == 0)
                size = jnp.int32(1)
                for _, same in twin[i]:
                    size = size + jnp.where(same, 1, 0)
                when = ready[i]
                for _ in range(slots - ROOM):
                    taken = jnp.int32(0)
                    for k in range(slots):
                        taken = taken + jnp.where(given[k] == when, 1, 0)
                    when = when + jnp.where(taken + size > ROOM, 1, 0)
                for k, same in twin[i]:
                    given[k] = jnp.where(wanted & same, when, given[k])
                given[i] = jnp.where(wanted, when, given[i])
        source = source_ref[...]
        lane = iota(source.shape, 1)
        for i in range(slots):
            here = layer * slots + i
            round_ref[here] = given[i]
            round2_ref[here] = given[i]
            most = jnp.maximum(most, given[i])
            ready_ref[token[i]] = jnp.where(live[i] > 0, given[i] + 1, ready_ref[token[i]])
            last_ref[token[i]] = jnp.where(live[i] > 0, here, last_ref[token[i]])
            source = jnp.where((lane == token[i]) & ((live[i] > 0) & (layer >= place)), here, source)
        source_ref[...] = source
        return most

    for i in range(slots):
        own_ref[i] = -1
    source_ref[...] = jnp.full(source_ref.shape, -1, I32)
    lax.fori_loop(0, sections, clear, 0)
    lax.fori_loop(0, sections, climb, 0)
    own_ref[slots] = lax.fori_loop(0, sections, descend, jnp.int32(1))
    for i in range(slots + 1):
        own2_ref[i] = own_ref[i]


def row_map(round_ref, sections, slots, start, news, table=False):
    block = sections * ROOM
    found = []
    for layer in range(sections):
        ranks = [jnp.int32(0)] * news
        for i in range(slots):
            k = layer * slots + i
            at = jnp.int32(start + news * block + k if table else -1)
            for b in range(news):
                hit = round_ref[k] == b + 1
                at = jnp.where(hit, start + b * block + layer * ROOM + ranks[b], at)
                ranks[b] = ranks[b] + jnp.where(hit, 1, 0)
            found.append(at)
    return found


def own_picks(round_ref, place, slots, now):
    picks = [jnp.int32(-1)] * ROOM
    rank = jnp.int32(0)
    for i in range(slots):
        hit = round_ref[place * slots + i] == now
        for c in range(ROOM):
            picks[c] = jnp.where(hit & (rank == c), i, picks[c])
        rank = rank + jnp.where(hit, 1, 0)
    return picks


def stacked(refs, part):
    rows = [r[:, :, part].reshape(r.shape[0] * r.shape[1], part.size) for r in refs]
    return jnp.concatenate(rows) if len(rows) > 1 else rows[0]


def send_kernel(sections, news, table, note, now_ref, place_ref, round_ref, own_ref, gate_ref, first_ref, *refs):
    held = refs[: news + table]
    sent_ref, row_in_ref, map_ref = refs[news + table :]
    cap = gate_ref.shape[2]
    slots, width = first_ref.shape
    now, place = now_ref[0], place_ref[0]
    for k, at in enumerate(row_map(round_ref, sections, slots, 0, news, table)):
        map_ref[k] = at
    wanted, from_first, weights = [], [], []
    for slot in own_picks(round_ref, place, slots, now):
        at = jnp.maximum(slot, 0)
        source = own_ref[at]
        wanted.append(jnp.where((slot >= 0) & (source >= 0), map_ref[jnp.maximum(source, 0)], -1))
        from_first.append(jnp.where((slot >= 0) & (source < 0), slot, -1))
        weights.append(jnp.where(slot >= 0, gate_ref[0, at // cap, at % cap], 0.0))
    weight = column(weights, (8, LANES))[:, :1]
    first_id = column(from_first, (8, LANES))
    in_first = [jnp.where(first_id == i, 1.0, 0.0)[:, :1] for i in range(slots)]
    if held:
        total = sum(r.shape[0] * r.shape[1] for r in held)
        ids = column(wanted, (8, total))
        pick = one_hot(ids == iota(ids.shape, 1))
    for part in chunks(width):
        first = first_ref[:, part].astype(F32)
        rows = dot(pick, stacked(held, part)) if held else jnp.zeros((8, part.size), F32)
        for i in range(slots):
            rows = rows + in_first[i] * first[i : i + 1]
        row_in_ref[:, part] = rows[:ROOM]
        scaled = (weight * rows)[:ROOM].astype(BF)
        for chip in range(sent_ref.shape[0]):
            sent_ref[chip, :, part] = scaled
    if note:
        lane = iota((ROOM, LANES), 1)
        word = jnp.zeros((ROOM, LANES), I32)
        for i in range(slots):
            word = jnp.where(lane == i, round_ref[place * slots + i], word)
        word = jnp.where(lane == slots, own_ref[slots], word).astype(F32).astype(BF)
        for chip in range(sent_ref.shape[0]):
            sent_ref[chip, :, pl.ds(width, LANES)] = word


def merge_kernel(now_ref, round_ref, table_ref, news_ref, merged_ref):
    sections, slots, width = table_ref.shape
    known, total = sections * slots, sections * (slots + ROOM)
    where_is = []
    for layer in range(sections):
        rank = jnp.int32(0)
        for i in range(slots):
            hit = round_ref[layer * slots + i] == now_ref[0]
            where_is.append(jnp.where(hit, known + layer * ROOM + rank, layer * slots + i))
            rank = rank + jnp.where(hit, 1, 0)
    pick = one_hot(column(where_is, (known, total)) == iota((known, total), 1))
    for part in chunks(width):
        rows = dot(pick, stacked([table_ref, news_ref], part))
        merged_ref[:, :, part] = rows.astype(BF).reshape(sections, slots, part.size)


def places(count, chips, cap, tok_group, core, taken):
    total = 2 * chips * count
    row = iota((total, LANES), 0)
    half = row // (chips * count)
    index = (row // count) % chips * 2 + (core ^ half)
    place = jnp.full((total, LANES), -1, I32)
    for i, flag in enumerate(taken):
        place = jnp.where(flag, (i // cap) * tok_group + index * cap + i % cap, place)
    return place


def pass_kernel(count, late, cap, core_ref, now_ref, saved_ref, down_ref, up_ref, own_ref, other_ref, *refs):
    refs = list(refs)
    note_in = refs.pop(0) if late == 2 else None
    mine_ref, theirs_ref, hidden_ref = refs[:3]
    chips = own_ref.shape[0]
    micros, group, hid = saved_ref.shape[1:]
    width = mine_ref.shape[2]
    half = chips * count
    core = core_ref[0]
    if late == 1:
        perm_ref, note_ref, later_ref, most_ref = refs[3:]
        lanes = pl.ds(width, LANES)
        word = jnp.concatenate([r[:, :, lanes].reshape(half, LANES) for r in (own_ref, other_ref)]).astype(F32)
        note_ref[...] = word
        later_ref[...] = word
        most_ref[0] = jnp.max(word).astype(I32)
    else:
        (perm_ref,) = refs[3:]
        word = note_in[...]
    now = now_ref[0].astype(F32)
    position = (iota((2 * half, 1), 0) % count).astype(F32)
    rank = jnp.zeros((2 * half, 1), F32)
    taken = []
    for i in range(micros * cap):
        hit = jnp.where(word[:, i : i + 1] == now, 1.0, 0.0)
        flag = jnp.where(rank == position, hit, 0.0)
        taken.append(jnp.broadcast_to(flag, (2 * half, LANES)) > 0.5)
        rank = rank + hit
    place = places(count, chips, cap, group, core, taken)
    perm = one_hot(place == iota(place.shape, 1))
    perm_ref[...] = perm
    v = dot(perm, saved_ref[0].reshape(micros * group, hid))
    s = 1.0 / (1.0 + jnp.exp(-v))
    slope = s * (1.0 + v * (1.0 - s))
    back = jnp.zeros((2 * half, hid), F32)
    for part in chunks(width):
        rows = jnp.concatenate(
            [own_ref[:, :, part].reshape(half, part.size), other_ref[:, :, part].reshape(half, part.size)]
        )
        back = back + dot(rows, down_ref[0, :, part], NT)
    hidden = (back * slope).astype(BF)
    hidden_ref[...] = hidden
    for part in chunks(width):
        partial = dot(hidden, up_ref[0, :, part])
        mine_ref[:, :, part] = partial[:half].reshape(chips, count, part.size)
        theirs_ref[:, :, part] = partial[half:].astype(BF).reshape(chips, count, part.size)


def news_kernel(now_ref, place_ref, round_ref, token_ref, row_in_ref, swapped_ref, news_ref):
    chips, count, width = swapped_ref.shape
    micros, cap = token_ref.shape[1:]
    ids = own_picks(round_ref, place_ref[0], micros * cap, now_ref[0])
    micro, token = [], []
    for c, slot in enumerate(ids):
        at = jnp.maximum(slot, 0)
        micro.append(jnp.where(slot >= 0, at // cap, -1 - c))
        token.append(token_ref[0, at // cap, at % cap])
    twins = []
    for b in range(count):
        same = [
            jnp.where((micro[a] == micro[b]) & (token[a] == token[b]), 1.0, 0.0) if a != b else jnp.float32(0.0)
            for a in range(count)
        ]
        twins.append(column(same, (count, LANES))[:, :1])
    for part in chunks(width):
        own = swapped_ref[0, :, part].astype(F32)
        for chip in range(1, chips):
            own = own + swapped_ref[chip, :, part].astype(F32)
        total = own
        for b in range(count):
            total = total + twins[b] * own[b : b + 1]
        rows = (row_in_ref[:, part] + total).astype(BF)
        for section in range(news_ref.shape[0]):
            news_ref[section, :, part] = rows


def grads_kernel(rounds, saved_t_ref, x_any, *refs):
    up_any, down_any, x_ref, up_ref, down_ref, sems = refs[-6:]
    hids, perms, owns, others = (refs[i : 4 * rounds : 4] for i in range(4))
    so_far = refs[4 * rounds : -6]
    natural = saved_t_ref.shape[1]
    width = x_ref.shape[2]
    parts = chunks(width)
    arriving = [
        pltpu.make_async_copy(x_any.at[0, :, :, part], x_ref.at[:, :, part], sems.at[n]) for n, part in enumerate(parts)
    ]
    for copy in arriving:
        copy.start()
    perm = jnp.concatenate([p[...] for p in perms])
    v = saved_t_ref[...].astype(F32)
    act = (v * (1.0 / (1.0 + jnp.exp(-v)))).astype(BF)
    act_rows = dot(act, perm, NT).astype(BF)
    hidden_t = dot(jnp.concatenate([h[...] for h in hids]), perm, TN).astype(BF)
    held = [r for pair in zip(owns, others) for r in pair]
    leaving = []
    for n, part in enumerate(parts):
        down = dot(act_rows, stacked(held, part))
        arriving[n].wait()
        up = dot(hidden_t, x_ref[:, :, part].reshape(natural, part.size))
        if so_far:
            up = up + so_far[0][0, :, part].astype(F32)
            down = down + so_far[1][0, :, part].astype(F32)
        down_ref[:, part] = down.astype(BF)
        up_ref[:, part] = up.astype(BF)
        for i, (a, b) in enumerate(((up_ref, up_any), (down_ref, down_any))):
            at = len(parts) * (1 + i) + n
            leaving.append(pltpu.make_async_copy(a.at[:, part], b.at[0, :, part], sems.at[at]))
            leaving[-1].start()
    for copy in leaving:
        copy.wait()


def output_kernel(round_ref, source_ref, grad_ref, *refs):
    held = [grad_ref, *refs[: UNROLLED + 1]]
    out_any, out_ref, sems = refs[UNROLLED + 1 :]
    sections, slots, width = held[-1].shape
    micros, tok_rows, _ = grad_ref.shape
    natural = micros * tok_rows
    source = source_ref[...]
    at = iota(source.shape, 1)
    for k, where_is in enumerate(row_map(round_ref, sections, slots, natural, UNROLLED, True)):
        at = jnp.where(source == k, where_is, at)
    total = sum(r.shape[0] * r.shape[1] for r in held)
    pick = one_hot(iota((total, natural), 0) == at)
    copies = []
    for n, part in enumerate(chunks(width)):
        out_ref[:, :, part] = dot(pick, stacked(held, part), TN).astype(BF).reshape(micros, tok_rows, part.size)
        copies.append(pltpu.make_async_copy(out_ref.at[:, :, part], out_any.at[0, :, :, part], sems.at[n]))
        copies[n].start()
    for copy in copies:
        copy.wait()


def per_device(out_grad, x_rows, saved_u, w_up_t, w_down, gate, route_tokens, route_count):
    sections = lax.axis_size("section")
    dp_count = lax.axis_size("dp")
    section_index = lax.axis_index("section")
    core = lax.axis_index("dp") % 2
    micros, tok_rows, width = out_grad.shape
    cap = gate.shape[2]
    hid = w_down.shape[1]
    chips = dp_count // 2
    slots = micros * cap
    same_core = [[2 * chip + c for chip in range(chips)] for c in range(2)]
    sibling = [(i, i ^ 1) for i in range(dp_count)]
    place = section_index.reshape(1).astype(I32)
    core_id = core.reshape(1).astype(I32)

    def shape(dims, dtype):
        return jax.ShapeDtypeStruct(dims, dtype)

    def swap(block, axis, groups=None):
        return lax.all_to_all(block, axis, 0, 0, tiled=True, axis_index_groups=groups)

    def number(n):
        return jnp.full((1,), n, I32)

    def in_vmem(block):
        return pltpu.with_memory_space_constraint(block, pltpu.VMEM)

    def send(now, note, rounds_of, own_plan, *held):
        news = min(len(held), UNROLLED)
        return call(
            functools.partial(send_kernel, sections, news, len(held) - news, note),
            [SMEM] * 5 + [VMEM] * (1 + len(held)),
            [shape((chips, ROOM, width + LANES * note), BF), shape((ROOM, width), F32)],
            [VMEM] * 2,
            [pltpu.SMEM((sections * slots,), I32)],
        )(now, place, rounds_of, own_plan, gate, first, *held)

    def one_pass(now, late, own, note=None):
        other = lax.ppermute(own, "dp", sibling)
        total = 2 * chips * ROOM
        outs = [shape((chips, ROOM, width), F32), shape((chips, ROOM, width), BF), shape((total, hid), BF)]
        outs.append(shape((total, LANES), BF))
        outs += [shape((total, LANES), F32)] * 2 + [shape((1,), I32)] if late == 1 else []
        mine, theirs, hidden, perm, *rest = call(
            functools.partial(pass_kernel, ROOM, late, cap),
            [SMEM, SMEM] + [VMEM] * (5 + (late == 2)),
            outs,
            [VMEM] * 4 + ([VMEM, VMEM, SMEM] if late == 1 else []),
            flops=4 * total * hid * width,
            size=4 * hid * width + 8 * total * width,
        )(core_id, now, saved_here, w_down, w_up_t, own, other, *([note] if late == 2 else []))
        arrived = lax.ppermute(theirs, "dp", sibling)
        pair_sum = (mine + arrived.astype(F32)).astype(BF)
        return swap(pair_sum, "dp", same_core), [hidden, perm, own, other], rest

    def make_news(now, rounds_of, row_in, swapped):
        return call(
            news_kernel,
            [SMEM] * 4 + [VMEM] * 2,
            shape((sections,) + swapped.shape[1:], BF),
            VMEM,
        )(now, place, rounds_of, route_tokens, row_in, swapped)

    def gradients(kept, so_far=()):
        return call(
            functools.partial(grads_kernel, len(kept)),
            [VMEM, ANY] + [VMEM] * (4 * len(kept) + len(so_far)),
            [shape((1, hid, width), BF)] * 2,
            [ANY] * 2,
            [pltpu.VMEM(x_rows.shape[1:], BF)]
            + [pltpu.VMEM((hid, width), BF)] * 2
            + [pltpu.SemaphoreType.DMA((3 * len(chunks(width)),))],
            flops=8 * dp_count * slots * hid * width,
            size=8 * hid * width,
        )(saved_t, pltpu.with_memory_space_constraint(x_rows, pltpu.HBM), *[a for one in kept for a in one], *so_far)

    info = call(info_kernel, [SMEM] * 2, shape((sections, 1, LANES), I32), VMEM)(
        route_tokens, route_count.transpose(0, 2, 1)
    )
    first = call(first_kernel, [SMEM, VMEM], shape((slots, width), BF), VMEM)(route_tokens, out_grad)
    info, first = lax.optimization_barrier((swap(info, "section"), first))
    rounds_of, own_plan, source, *again_plan = call(
        functools.partial(plan_kernel, sections, cap, tok_rows),
        [SMEM, SMEM],
        [shape((sections * slots,), I32), shape((slots + 1,), I32), shape((1, micros * tok_rows), I32)]
        + [shape((sections * slots,), I32), shape((slots + 1,), I32)],
        [SMEM, SMEM, VMEM, SMEM, SMEM],
        [pltpu.SMEM((micros * tok_rows,), I32)] * 3 + [pltpu.SMEM((sections * slots,), I32)],
    )(info, place)
    saved_t = saved_u.reshape(micros * dp_count * cap, hid).T
    saved_here = in_vmem(saved_u)

    sent, row_in = send(number(1), True, rounds_of, own_plan)
    swapped, kept1, (note, note_later, most) = one_pass(number(1), 1, swap(sent, "dp", same_core))
    news1 = swap(make_news(number(1), rounds_of, row_in, swapped), "section")
    sent, row_in = send(number(2), False, rounds_of, own_plan, news1)
    swapped, kept2, _ = one_pass(number(2), 2, swap(sent, "dp", same_core), note)
    news2 = swap(make_news(number(2), rounds_of, row_in, swapped), "section")
    sent, row_in = send(number(3), False, rounds_of, own_plan, news1, news2)
    swapped, kept3, _ = one_pass(number(3), 2, swap(sent, "dp", same_core), note)
    news3 = make_news(number(3), rounds_of, row_in, swapped)
    news3, *grads = lax.optimization_barrier((swap(news3, "section"), *gradients([kept1, kept2, kept3])))

    def more(state):
        return state[0] < most[0]

    def again(state):
        done, table, *grads = state
        now = (done + 1).reshape(1)
        sent, row_in = send(now, False, *again_plan, news1, news2, news3, table)
        swapped, kept, _ = one_pass(now, 2, swap(sent, "dp", same_core), note_later)
        news = swap(make_news(now, again_plan[0], row_in, swapped), "section")
        table = call(merge_kernel, [SMEM] * 2 + [VMEM] * 2, shape(table.shape, BF), VMEM)(now, again_plan[0], table, news)
        return done + 1, table, *gradients([kept], grads)

    table = jnp.zeros((sections, slots, width), BF)
    _, table, grad_up, grad_down = lax.while_loop(more, again, (jnp.int32(UNROLLED), table, *grads))
    in_grad = call(
        output_kernel,
        [SMEM] + [VMEM] * (3 + UNROLLED),
        shape((1, micros, tok_rows, width), BF),
        ANY,
        [pltpu.VMEM(out_grad.shape, BF), pltpu.SemaphoreType.DMA((len(chunks(width)),))],
    )(again_plan[0], source, out_grad, news1, news2, news3, table)
    return (in_grad, grad_up, grad_down)


def solution(mesh):
    return jax.shard_map(
        per_device,
        mesh=mesh,
        in_specs=(
            P(None, "dp", None),
            P("section", None, None, None),
            P("section", None, None, "dp"),
            P("section", "dp", None),
            P("section", "dp", None),
            P("section", None, "dp"),
            P("section", None, "dp"),
            P("section", None, "dp"),
        ),
        out_specs=(
            P("section", None, "dp", None),
            P("section", "dp", None),
            P("section", "dp", None),
        ),
        check_vma=False,
    )
```

```python
import functools

import jax
import jax.numpy as jnp
from jax import lax
from jax.experimental import pallas as pl
from jax.experimental.pallas import tpu as pltpu
from jax.sharding import PartitionSpec as P

BF = jnp.bfloat16
F32 = jnp.float32
I32 = jnp.int32
LANES = 128
ROOM = 2
UNROLLED = 3
NT = (((1,), (1,)), ((), ()))
TN = (((0,), (0,)), ((), ()))
SMEM = pl.BlockSpec(memory_space=pltpu.SMEM)
VMEM = pl.BlockSpec(memory_space=pltpu.VMEM)
ANY = pl.BlockSpec(memory_space=pl.ANY)


def call(kernel, ins, outs, out_specs, scratch=(), flops=1000000, size=1000000):
    return pl.pallas_call(
        kernel,
        in_specs=ins,
        out_specs=out_specs,
        out_shape=outs,
        scratch_shapes=list(scratch),
        compiler_params=pltpu.CompilerParams(vmem_limit_bytes=24 * 1024 * 1024),
        cost_estimate=pl.CostEstimate(flops=flops, bytes_accessed=size, transcendentals=0),
    )


def chunks(width):
    step = next(s for s in (1024, 768, 512, 384, 256, 128) if width % s == 0)
    return [pl.ds(at, step) for at in range(0, width, step)]


def dot(a, b, dims=None):
    if dims is None:
        return jnp.dot(a, b, preferred_element_type=F32)
    return lax.dot_general(a, b, dims, preferred_element_type=F32)


def iota(shape, axis):
    return lax.broadcasted_iota(I32, shape, axis)


def one_hot(flag):
    return jnp.where(flag, 1.0, 0.0).astype(BF)


def column(values, shape):
    rows = iota(shape, 0)
    out = jnp.full(shape, values[0])
    for i in range(1, len(values)):
        out = jnp.where(rows == i, values[i], out)
    return out


def info_kernel(token_ref, count_ref, info_ref):
    micros, cap = token_ref.shape[1:]
    slots = micros * cap
    lane = iota((1, LANES), 1)
    info = jnp.zeros((1, LANES), I32)
    for i in range(slots):
        live = jnp.where(i % cap < count_ref[0, 0, i // cap], 1, 0)
        info = jnp.where(lane == i, token_ref[0, i // cap, i % cap], info)
        info = jnp.where(lane == slots + i, live, info)
    for section in range(info_ref.shape[0]):
        info_ref[section] = info


def first_kernel(token_ref, grad_ref, first_ref):
    micros, tok_rows, width = grad_ref.shape
    cap = token_ref.shape[2]
    slots = micros * cap
    tokens = [token_ref[0, i // cap, i % cap] + (i // cap) * tok_rows for i in range(slots)]
    wanted = column(tokens, (8, micros * tok_rows))
    pick = one_hot(wanted == iota(wanted.shape, 1))
    for part in chunks(width):
        rows = dot(pick, grad_ref[:, :, part].reshape(micros * tok_rows, part.size))
        first_ref[:, part] = rows[:slots].astype(BF)


def plan_kernel(sections, cap, tok_rows, info_ref, place_ref, round_ref, own_ref, source_ref, round2_ref, own2_ref, ready_ref, last_ref, below_ref, height_ref):
    slots = 2 * cap
    place = place_ref[0]

    def routed(layer):
        token = [info_ref[layer, 0, i] + (i // cap) * tok_rows for i in range(slots)]
        live = [info_ref[layer, 0, slots + i] for i in range(slots)]
        return token, live

    def mates(i):
        return [k for k in range(i // cap * cap, i // cap * cap + cap) if k != i]

    def clear(layer, carry):
        for token in routed(layer)[0]:
            ready_ref[token] = 1
            last_ref[token] = -1
            below_ref[token] = 0
        return carry

    def climb(layer, carry):
        token, live = routed(layer)
        for i in range(slots):
            height_ref[layer * slots + i] = below_ref[token[i]]
        for i in range(slots):
            new = live[i]
            for k in mates(i):
                if k < i:
                    new = jnp.where((token[k] == token[i]) & (live[k] > 0), 0, new)
            below_ref[token[i]] = below_ref[token[i]] + new
        return carry

    def descend(step, most):
        layer = sections - 1 - step
        token, live = routed(layer)
        own = layer == place
        for i in range(slots):
            own_ref[i] = jnp.where(own, last_ref[token[i]], own_ref[i])
        height = [height_ref[layer * slots + i] for i in range(slots)]
        ready = [ready_ref[token[i]] for i in range(slots)]
        twin = [
            [(k, (token[k] == token[i]) & (live[k] > 0)) for k in mates(i)] for i in range(slots)
        ]
        given = [jnp.int32(0)] * slots
        for awaited in (True, False):
            for i in range(slots):
                wanted = (height[i] > 0) if awaited else (height[i] == 0)
                wanted = wanted & (live[i] > 0) & (given[i] == 0)
                size = jnp.int32(1)
                for _, same in twin[i]:
                    size = size + jnp.where(same, 1, 0)
                when = ready[i]
                for _ in range(slots - ROOM):
                    taken = jnp.int32(0)
                    for k in range(slots):
                        taken = taken + jnp.where(given[k] == when, 1, 0)
                    when = when + jnp.where(taken + size > ROOM, 1, 0)
                for k, same in twin[i]:
                    given[k] = jnp.where(wanted & same, when, given[k])
                given[i] = jnp.where(wanted, when, given[i])
        source = source_ref[...]
        lane = iota(source.shape, 1)
        for i in range(slots):
            here = layer * slots + i
            round_ref[here] = given[i]
            round2_ref[here] = given[i]
            most = jnp.maximum(most, given[i])
            ready_ref[token[i]] = jnp.where(live[i] > 0, given[i] + 1, ready_ref[token[i]])
            last_ref[token[i]] = jnp.where(live[i] > 0, here, last_ref[token[i]])
            source = jnp.where((lane == token[i]) & ((live[i] > 0) & (layer >= place)), here, source)
        source_ref[...] = source
        return most

    for i in range(slots):
        own_ref[i] = -1
    source_ref[...] = jnp.full(source_ref.shape, -1, I32)
    most = jnp.int32(1)
    for layer in range(sections):
        clear(layer, 0)
    for layer in range(sections):
        climb(layer, 0)
    for step in range(sections):
        most = descend(step, most)
    own_ref[slots] = most
    for i in range(slots + 1):
        own2_ref[i] = own_ref[i]


def row_map(round_ref, sections, slots, start, news, table=False):
    block = sections * ROOM
    found = []
    for layer in range(sections):
        ranks = [jnp.int32(0)] * news
        for i in range(slots):
            k = layer * slots + i
            at = jnp.int32(start + news * block + k if table else -1)
            for b in range(news):
                hit = round_ref[k] == b + 1
                at = jnp.where(hit, start + b * block + layer * ROOM + ranks[b], at)
                ranks[b] = ranks[b] + jnp.where(hit, 1, 0)
            found.append(at)
    return found


def own_picks(round_ref, place, slots, now):
    picks = [jnp.int32(-1)] * ROOM
    rank = jnp.int32(0)
    for i in range(slots):
        hit = round_ref[place * slots + i] == now
        for c in range(ROOM):
            picks[c] = jnp.where(hit & (rank == c), i, picks[c])
        rank = rank + jnp.where(hit, 1, 0)
    return picks


def stacked(refs, part):
    rows = [r[:, :, part].reshape(r.shape[0] * r.shape[1], part.size) for r in refs]
    return jnp.concatenate(rows) if len(rows) > 1 else rows[0]


def send_kernel(sections, news, table, note, now_ref, place_ref, round_ref, own_ref, gate_ref, first_ref, *refs):
    held = refs[: news + table]
    sent_ref, row_in_ref, map_ref = refs[news + table :]
    cap = gate_ref.shape[2]
    slots, width = first_ref.shape
    now, place = now_ref[0], place_ref[0]
    for k, at in enumerate(row_map(round_ref, sections, slots, 0, news, table)):
        map_ref[k] = at
    wanted, from_first, weights = [], [], []
    for slot in own_picks(round_ref, place, slots, now):
        at = jnp.maximum(slot, 0)
        source = own_ref[at]
        wanted.append(jnp.where((slot >= 0) & (source >= 0), map_ref[jnp.maximum(source, 0)], -1))
        from_first.append(jnp.where((slot >= 0) & (source < 0), slot, -1))
        weights.append(jnp.where(slot >= 0, gate_ref[0, at // cap, at % cap], 0.0))
    weight = column(weights, (8, LANES))[:, :1]
    first_id = column(from_first, (8, LANES))
    in_first = [jnp.where(first_id == i, 1.0, 0.0)[:, :1] for i in range(slots)]
    if held:
        total = sum(r.shape[0] * r.shape[1] for r in held)
        ids = column(wanted, (8, total))
        pick = one_hot(ids == iota(ids.shape, 1))
    for part in chunks(width):
        first = first_ref[:, part].astype(F32)
        rows = dot(pick, stacked(held, part)) if held else jnp.zeros((8, part.size), F32)
        for i in range(slots):
            rows = rows + in_first[i] * first[i : i + 1]
        row_in_ref[:, part] = rows[:ROOM]
        scaled = (weight * rows)[:ROOM].astype(BF)
        for chip in range(sent_ref.shape[0]):
            sent_ref[chip, :, part] = scaled
    if note:
        lane = iota((ROOM, LANES), 1)
        word = jnp.zeros((ROOM, LANES), I32)
        for i in range(slots):
            word = jnp.where(lane == i, round_ref[place * slots + i], word)
        word = jnp.where(lane == slots, own_ref[slots], word).astype(F32).astype(BF)
        for chip in range(sent_ref.shape[0]):
            sent_ref[chip, :, pl.ds(width, LANES)] = word


def merge_kernel(now_ref, round_ref, table_ref, news_ref, merged_ref):
    sections, slots, width = table_ref.shape
    known, total = sections * slots, sections * (slots + ROOM)
    where_is = []
    for layer in range(sections):
        rank = jnp.int32(0)
        for i in range(slots):
            hit = round_ref[layer * slots + i] == now_ref[0]
            where_is.append(jnp.where(hit, known + layer * ROOM + rank, layer * slots + i))
            rank = rank + jnp.where(hit, 1, 0)
    pick = one_hot(column(where_is, (known, total)) == iota((known, total), 1))
    for part in chunks(width):
        rows = dot(pick, stacked([table_ref, news_ref], part))
        merged_ref[:, :, part] = rows.astype(BF).reshape(sections, slots, part.size)


def places(count, chips, cap, tok_group, core, taken):
    total = 2 * chips * count
    row = iota((total, LANES), 0)
    half = row // (chips * count)
    index = (row // count) % chips * 2 + (core ^ half)
    place = jnp.full((total, LANES), -1, I32)
    for i, flag in enumerate(taken):
        place = jnp.where(flag, (i // cap) * tok_group + index * cap + i % cap, place)
    return place


def pass_kernel(count, late, cap, core_ref, now_ref, saved_ref, down_ref, up_ref, own_ref, other_ref, *refs):
    refs = list(refs)
    note_in = refs.pop(0) if late == 2 else None
    mine_ref, theirs_ref, hidden_ref = refs[:3]
    chips = own_ref.shape[0]
    micros, group, hid = saved_ref.shape[1:]
    width = mine_ref.shape[2]
    half = chips * count
    core = core_ref[0]
    if late == 1:
        perm_ref, note_ref, later_ref, most_ref = refs[3:]
        lanes = pl.ds(width, LANES)
        word = jnp.concatenate([r[:, :, lanes].reshape(half, LANES) for r in (own_ref, other_ref)]).astype(F32)
        note_ref[...] = word
        later_ref[...] = word
        most_ref[0] = jnp.max(word).astype(I32)
    else:
        (perm_ref,) = refs[3:]
        word = note_in[...]
    now = now_ref[0].astype(F32)
    position = (iota((2 * half, 1), 0) % count).astype(F32)
    rank = jnp.zeros((2 * half, 1), F32)
    taken = []
    for i in range(micros * cap):
        hit = jnp.where(word[:, i : i + 1] == now, 1.0, 0.0)
        flag = jnp.where(rank == position, hit, 0.0)
        taken.append(jnp.broadcast_to(flag, (2 * half, LANES)) > 0.5)
        rank = rank + hit
    place = places(count, chips, cap, group, core, taken)
    perm = one_hot(place == iota(place.shape, 1))
    perm_ref[...] = perm
    v = dot(perm, saved_ref[0].reshape(micros * group, hid))
    s = 1.0 / (1.0 + jnp.exp(-v))
    slope = s * (1.0 + v * (1.0 - s))
    back = jnp.zeros((2 * half, hid), F32)
    for part in chunks(width):
        rows = jnp.concatenate(
            [own_ref[:, :, part].reshape(half, part.size), other_ref[:, :, part].reshape(half, part.size)]
        )
        back = back + dot(rows, down_ref[0, :, part], NT)
    hidden = (back * slope).astype(BF)
    hidden_ref[...] = hidden
    for part in chunks(width):
        partial = dot(hidden, up_ref[0, :, part])
        mine_ref[:, :, part] = partial[:half].reshape(chips, count, part.size)
        theirs_ref[:, :, part] = partial[half:].astype(BF).reshape(chips, count, part.size)


def news_kernel(now_ref, place_ref, round_ref, token_ref, row_in_ref, swapped_ref, news_ref):
    chips, count, width = swapped_ref.shape
    micros, cap = token_ref.shape[1:]
    ids = own_picks(round_ref, place_ref[0], micros * cap, now_ref[0])
    micro, token = [], []
    for c, slot in enumerate(ids):
        at = jnp.maximum(slot, 0)
        micro.append(jnp.where(slot >= 0, at // cap, -1 - c))
        token.append(token_ref[0, at // cap, at % cap])
    twins = []
    for b in range(count):
        same = [
            jnp.where((micro[a] == micro[b]) & (token[a] == token[b]), 1.0, 0.0) if a != b else jnp.float32(0.0)
            for a in range(count)
        ]
        twins.append(column(same, (count, LANES))[:, :1])
    for part in chunks(width):
        own = swapped_ref[0, :, part].astype(F32)
        for chip in range(1, chips):
            own = own + swapped_ref[chip, :, part].astype(F32)
        total = own
        for b in range(count):
            total = total + twins[b] * own[b : b + 1]
        rows = (row_in_ref[:, part] + total).astype(BF)
        for section in range(news_ref.shape[0]):
            news_ref[section, :, part] = rows


def grads_kernel(rounds, saved_t_ref, x_any, *refs):
    up_any, down_any, x_ref, up_ref, down_ref, sems = refs[-6:]
    hids, perms, owns, others = (refs[i : 4 * rounds : 4] for i in range(4))
    so_far = refs[4 * rounds : -6]
    natural = saved_t_ref.shape[1]
    width = x_ref.shape[2]
    parts = chunks(width)
    arriving = [
        pltpu.make_async_copy(x_any.at[0, :, :, part], x_ref.at[:, :, part], sems.at[n]) for n, part in enumerate(parts)
    ]
    for copy in arriving:
        copy.start()
    perm = jnp.concatenate([p[...] for p in perms])
    v = saved_t_ref[...].astype(F32)
    act = (v * (1.0 / (1.0 + jnp.exp(-v)))).astype(BF)
    act_rows = dot(act, perm, NT).astype(BF)
    hidden_t = dot(jnp.concatenate([h[...] for h in hids]), perm, TN).astype(BF)
    held = [r for pair in zip(owns, others) for r in pair]
    leaving = []
    for n, part in enumerate(parts):
        down = dot(act_rows, stacked(held, part))
        arriving[n].wait()
        up = dot(hidden_t, x_ref[:, :, part].reshape(natural, part.size))
        if so_far:
            up = up + so_far[0][0, :, part].astype(F32)
            down = down + so_far[1][0, :, part].astype(F32)
        down_ref[:, part] = down.astype(BF)
        up_ref[:, part] = up.astype(BF)
        for i, (a, b) in enumerate(((up_ref, up_any), (down_ref, down_any))):
            at = len(parts) * (1 + i) + n
            leaving.append(pltpu.make_async_copy(a.at[:, part], b.at[0, :, part], sems.at[at]))
            leaving[-1].start()
    for copy in leaving:
        copy.wait()


def output_kernel(round_ref, source_ref, grad_ref, *refs):
    held = [grad_ref, *refs[: UNROLLED + 1]]
    out_any, out_ref, sems = refs[UNROLLED + 1 :]
    sections, slots, width = held[-1].shape
    micros, tok_rows, _ = grad_ref.shape
    natural = micros * tok_rows
    source = source_ref[...]
    at = iota(source.shape, 1)
    for k, where_is in enumerate(row_map(round_ref, sections, slots, natural, UNROLLED, True)):
        at = jnp.where(source == k, where_is, at)
    total = sum(r.shape[0] * r.shape[1] for r in held)
    pick = one_hot(iota((total, natural), 0) == at)
    pick = dot(pick, one_hot(iota((total, total), 0) == iota((total, total), 1)), TN).astype(BF)
    copies = []
    for n, part in enumerate(chunks(width)):
        out_ref[:, :, part] = dot(pick, stacked(held, part)).astype(BF).reshape(micros, tok_rows, part.size)
        copies.append(pltpu.make_async_copy(out_ref.at[:, :, part], out_any.at[0, :, :, part], sems.at[n]))
        copies[n].start()
    for copy in copies:
        copy.wait()


def per_device(out_grad, x_rows, saved_u, w_up_t, w_down, gate, route_tokens, route_count):
    sections = lax.axis_size("section")
    dp_count = lax.axis_size("dp")
    section_index = lax.axis_index("section")
    core = lax.axis_index("dp") % 2
    micros, tok_rows, width = out_grad.shape
    cap = gate.shape[2]
    hid = w_down.shape[1]
    chips = dp_count // 2
    slots = micros * cap
    same_core = [[2 * chip + c for chip in range(chips)] for c in range(2)]
    sibling = [(i, i ^ 1) for i in range(dp_count)]
    place = section_index.reshape(1).astype(I32)
    core_id = core.reshape(1).astype(I32)

    def shape(dims, dtype):
        return jax.ShapeDtypeStruct(dims, dtype)

    def swap(block, axis, groups=None):
        return lax.all_to_all(block, axis, 0, 0, tiled=True, axis_index_groups=groups)

    def number(n):
        return jnp.full((1,), n, I32)

    def in_vmem(block):
        return pltpu.with_memory_space_constraint(block, pltpu.VMEM)

    def send(now, note, rounds_of, own_plan, *held):
        news = min(len(held), UNROLLED)
        return call(
            functools.partial(send_kernel, sections, news, len(held) - news, note),
            [SMEM] * 5 + [VMEM] * (1 + len(held)),
            [shape((chips, ROOM, width + LANES * note), BF), shape((ROOM, width), F32)],
            [VMEM] * 2,
            [pltpu.SMEM((sections * slots,), I32)],
        )(now, place, rounds_of, own_plan, gate, first, *held)

    def one_pass(now, late, own, note=None):
        other = lax.ppermute(own, "dp", sibling)
        total = 2 * chips * ROOM
        outs = [shape((chips, ROOM, width), F32), shape((chips, ROOM, width), BF), shape((total, hid), BF)]
        outs.append(shape((total, LANES), BF))
        outs += [shape((total, LANES), F32)] * 2 + [shape((1,), I32)] if late == 1 else []
        mine, theirs, hidden, perm, *rest = call(
            functools.partial(pass_kernel, ROOM, late, cap),
            [SMEM, SMEM] + [VMEM] * (5 + (late == 2)),
            outs,
            [VMEM] * 4 + ([VMEM, VMEM, SMEM] if late == 1 else []),
            flops=4 * total * hid * width,
            size=4 * hid * width + 8 * total * width,
        )(core_id, now, saved_here, w_down, w_up_t, own, other, *([note] if late == 2 else []))
        arrived = lax.ppermute(theirs, "dp", sibling)
        pair_sum = (mine + arrived.astype(F32)).astype(BF)
        return swap(pair_sum, "dp", same_core), [hidden, perm, own, other], rest

    def make_news(now, rounds_of, row_in, swapped):
        return call(
            news_kernel,
            [SMEM] * 4 + [VMEM] * 2,
            shape((sections,) + swapped.shape[1:], BF),
            VMEM,
        )(now, place, rounds_of, route_tokens, row_in, swapped)

    def gradients(kept, so_far=()):
        return call(
            functools.partial(grads_kernel, len(kept)),
            [VMEM, ANY] + [VMEM] * (4 * len(kept) + len(so_far)),
            [shape((1, hid, width), BF)] * 2,
            [ANY] * 2,
            [pltpu.VMEM(x_rows.shape[1:], BF)]
            + [pltpu.VMEM((hid, width), BF)] * 2
            + [pltpu.SemaphoreType.DMA((3 * len(chunks(width)),))],
            flops=8 * dp_count * slots * hid * width,
            size=8 * hid * width,
        )(saved_t, pltpu.with_memory_space_constraint(x_rows, pltpu.HBM), *[a for one in kept for a in one], *so_far)

    info = call(info_kernel, [SMEM] * 2, shape((sections, 1, LANES), I32), VMEM)(
        route_tokens, route_count.transpose(0, 2, 1)
    )
    first = call(first_kernel, [SMEM, VMEM], shape((slots, width), BF), VMEM)(route_tokens, out_grad)
    info, first = lax.optimization_barrier((swap(info, "section"), first))
    rounds_of, own_plan, source, *again_plan = call(
        functools.partial(plan_kernel, sections, cap, tok_rows),
        [SMEM, SMEM],
        [shape((sections * slots,), I32), shape((slots + 1,), I32), shape((1, micros * tok_rows), I32)]
        + [shape((sections * slots,), I32), shape((slots + 1,), I32)],
        [SMEM, SMEM, VMEM, SMEM, SMEM],
        [pltpu.SMEM((micros * tok_rows,), I32)] * 3 + [pltpu.SMEM((sections * slots,), I32)],
    )(info, place)
    saved_t = saved_u.reshape(micros * dp_count * cap, hid).T
    saved_here = in_vmem(saved_u)

    sent, row_in = send(number(1), True, rounds_of, own_plan)
    swapped, kept1, (note, note_later, most) = one_pass(number(1), 1, swap(sent, "dp", same_core))
    news1 = swap(make_news(number(1), rounds_of, row_in, swapped), "section")
    sent, row_in = send(number(2), False, rounds_of, own_plan, news1)
    swapped, kept2, _ = one_pass(number(2), 2, swap(sent, "dp", same_core), note)
    news2 = swap(make_news(number(2), rounds_of, row_in, swapped), "section")
    sent, row_in = send(number(3), False, rounds_of, own_plan, news1, news2)
    swapped, kept3, _ = one_pass(number(3), 2, swap(sent, "dp", same_core), note)
    news3 = make_news(number(3), rounds_of, row_in, swapped)
    news3, *grads = lax.optimization_barrier((swap(news3, "section"), *gradients([kept1, kept2, kept3])))

    def more(state):
        return state[0] < most[0]

    def again(state):
        done, table, *grads = state
        now = (done + 1).reshape(1)
        sent, row_in = send(now, False, *again_plan, news1, news2, news3, table)
        swapped, kept, _ = one_pass(now, 2, swap(sent, "dp", same_core), note_later)
        news = swap(make_news(now, again_plan[0], row_in, swapped), "section")
        table = call(merge_kernel, [SMEM] * 2 + [VMEM] * 2, shape(table.shape, BF), VMEM)(now, again_plan[0], table, news)
        return done + 1, table, *gradients([kept], grads)

    table = jnp.zeros((sections, slots, width), BF)
    _, table, grad_up, grad_down = lax.while_loop(more, again, (jnp.int32(UNROLLED), table, *grads))
    in_grad = call(
        output_kernel,
        [SMEM] + [VMEM] * (3 + UNROLLED),
        shape((1, micros, tok_rows, width), BF),
        ANY,
        [pltpu.VMEM(out_grad.shape, BF), pltpu.SemaphoreType.DMA((len(chunks(width)),))],
    )(again_plan[0], source, out_grad, news1, news2, news3, table)
    return (in_grad, grad_up, grad_down)


def solution(mesh):
    return jax.shard_map(
        per_device,
        mesh=mesh,
        in_specs=(
            P(None, "dp", None),
            P("section", None, None, None),
            P("section", None, None, "dp"),
            P("section", "dp", None),
            P("section", "dp", None),
            P("section", None, "dp"),
            P("section", None, "dp"),
            P("section", None, "dp"),
        ),
        out_specs=(
            P("section", None, "dp", None),
            P("section", "dp", None),
            P("section", "dp", None),
        ),
        check_vma=False,
    )
```
